32 devices in a mesh: groups: 2 (over x), gx: 2 (over core), gy: 8 (over z, y).
Axes of the slice: x: 2, y: 2, z: 4, core: 2. Of those that a mesh axis runs over, the one named last changes fastest.
Arguments:
- tokens: bfloat16 [1024, 8192], P(('groups', 'gy'), 'gx'), parts along dimension 0, may hold values from -6 to 6
- gate_weight: bfloat16 [8192, 16384], P('gx', 'gy'), may hold values from -0.0625 to 0.0625
- up_weight: bfloat16 [8192, 16384], P('gx', 'gy'), may hold values from -0.0625 to 0.0625
- down_weight: bfloat16 [16384, 8192], P('gy', 'gx'), may hold values from -0.046875 to 0.046875
Outputs:
- block_out: bfloat16 [1024, 8192], P(('groups', 'gy'), 'gx'), parts along dimension 0
The draws below stay inside these ranges and needn't reach their ends.
There are 2 independent parts, one for each index of `groups`. The reference program is written for one: setup_inputs(seed, part) draws one part's arguments, and reference() takes and returns one part's arrays. A program takes and returns all parts, laid end to end along the dimension named above; an argument that names none is the same for every part. Nothing has to cross between parts.
All inputs are finite; a program needn't handle non-finite values.
Results may differ from the reference program's by a relative error of at most 0.005.
Values may be sent and summed in bfloat16 or wider, within the bound.
No kernel may reach another device: no remote copies, remote signals or barrier semaphores. Data moves between devices by JAX's collectives and lax.ppermute only.
A program may use at most 192 MiB of HBM per device.

```python
import jax
import jax.numpy as jnp

D = 8192
FF = 16384
TOKENS = 512


def level_of(rng, dims, split, least, high):
    gain, own = 1.0, jax.random.fold_in(rng, 6)
    for position, parts in split:
        steps = jnp.exp(jax.random.uniform(jax.random.fold_in(own, position), (parts,), jnp.float32, least / len(split), high / len(split)))
        gain = gain * jnp.repeat(steps, dims[position] // parts).reshape([-1 if axis == position else 1 for axis in range(len(dims))])
    return gain


def scatter_about(own_key, dims, scale, most, pieces=(), held_as=jnp.bfloat16):
    drawn = jax.random.normal(own_key, dims, jnp.float32) * scale
    if len(pieces) > 0:
        drawn = level_of(own_key, dims, pieces, -0.22, 0.18) * drawn
    return jnp.clip(drawn, min=-most, max=most).astype(held_as)


def setup_inputs(seed: int = 0, part: int = 0) -> dict:
    splits = jax.random.split(jax.random.key(seed), 5)
    own_keys = jax.random.split(jax.random.fold_in(splits[4], part), 5)
    return {
        "tokens": scatter_about(own_keys[0], (TOKENS, D), 1.0, 6.0, ((0, 8), (1, 2))),
        "gate_weight": scatter_about(splits[1], (D, FF), D ** -0.5, 0.0625, ((0, 2), (1, 8))),
        "up_weight": scatter_about(splits[2], (D, FF), D ** -0.5, 0.0625, ((0, 2), (1, 8))),
        "down_weight": scatter_about(splits[3], (FF, D), FF ** -0.5, 0.046875, ((0, 8), (1, 2))),
    }


def reference(tokens, gate_weight, up_weight, down_weight):
    gate = jnp.dot(tokens, gate_weight, preferred_element_type=jnp.float32)
    up = jnp.dot(tokens, up_weight, preferred_element_type=jnp.float32)
    hidden = (jax.nn.silu(gate) * up).astype(jnp.bfloat16)
    return jnp.dot(hidden, down_weight, preferred_element_type=jnp.float32).astype(jnp.bfloat16)
```

```python
import jax
import jax.numpy as jnp
from jax import lax
from jax.sharding import PartitionSpec as P

F32, BF16 = jnp.float32, jnp.bfloat16


def ring_of(n):
    return list(range(0, n, 2)) + list(range(n - 1, 0, -2))


def make_shards(n):
    ring = ring_of(n)
    half = n // 2
    to_right = [(ring[i], ring[(i + 1) % n]) for i in range(n)]
    to_left = [(ring[(i + 1) % n], ring[i]) for i in range(n)]
    swap = [(0, 1), (1, 0)]

    def right(x):
        return lax.ppermute(x, "gy", to_right)

    def left(x):
        return lax.ppermute(x, "gy", to_left)

    def other(x):
        return lax.ppermute(x, "gx", swap)

    def shards(tokens, gate_weight, up_weight, down_weight):
        rows = tokens.shape[0]
        cut = rows // 2
        core = lax.axis_index("gx")
        first = core == 0

        blocks = [[tokens]]
        r = l = tokens
        for d in range(1, half):
            r, l = right(r), left(l)
            blocks.append([r, l])
        blocks.append([right(r[:cut]), left(l[cut:])])

        spans = [[0, 1]] + [[d] for d in range(2, half - 1)] + [[half - 1, half]]
        partial = {}
        for span in spans:
            x = jnp.concatenate([b for d in span for b in blocks[d]], axis=0)
            g = jnp.dot(x, gate_weight, preferred_element_type=F32)
            u = jnp.dot(x, up_weight, preferred_element_type=F32)
            w = g.shape[1] // 2
            low = jnp.stack([g[:, :w], u[:, :w]])
            high = jnp.stack([g[:, w:], u[:, w:]])
            mine = jnp.where(first, low, high)
            got = other(jnp.where(first, high, low))
            both = mine + got
            h = (jax.nn.silu(both[0]) * both[1]).astype(BF16)
            o = other(h)
            hidden = jnp.concatenate(
                [jnp.where(first, h, o), jnp.where(first, o, h)], axis=1
            )
            out = jnp.dot(hidden, down_weight, preferred_element_type=F32)
            at = 0
            for d in span:
                pieces = []
                for b in blocks[d]:
                    pieces.append(out[at : at + b.shape[0]])
                    at += b.shape[0]
                partial[d] = pieces

        back_l, back_r = partial[half]
        l = left(back_l.astype(BF16))
        r = right(back_r.astype(BF16))
        for d in range(half - 1, 0, -1):
            pl_, pr_ = partial[d]
            if d == half - 1:
                sl = jnp.concatenate([pl_[:cut] + l.astype(F32), pl_[cut:]], axis=0)
                sr = jnp.concatenate([pr_[:cut], pr_[cut:] + r.astype(F32)], axis=0)
            else:
                sl = pl_ + l.astype(F32)
                sr = pr_ + r.astype(F32)
            l, r = left(sl.astype(BF16)), right(sr.astype(BF16))
        total = partial[0][0] + l.astype(F32) + r.astype(F32)
        return total.astype(BF16)

    return shards


def solution(mesh):
    return jax.shard_map(
        make_shards(mesh.shape["gy"]),
        mesh=mesh,
        in_specs=(P(("groups", "gy"), "gx"), P("gx", "gy"), P("gx", "gy"), P("gy", "gx")),
        out_specs=P(("groups", "gy"), "gx"),
        check_vma=False,
    )
```

```python
import functools

import jax
import jax.numpy as jnp
from jax import lax
from jax.experimental import pallas as pl
from jax.experimental.pallas import tpu as pltpu
from jax.sharding import PartitionSpec as P

F32, BF16 = jnp.float32, jnp.bfloat16
VMEM = pl.BlockSpec(memory_space=pltpu.VMEM)
ANY = pl.BlockSpec(memory_space=pl.ANY)
SMEM = pl.BlockSpec(memory_space=pltpu.SMEM)


def ring_of(n):
    return list(range(0, n, 2)) + list(range(n - 1, 0, -2))


def held(x, after):
    for t in after:
        t = t[(0,) * t.ndim]
        x = jnp.where(t == t, x, t.astype(x.dtype))
    return x


def bring(w, after, parts=8):
    step = w.shape[0] // parts

    def body(w_ref, *refs):
        o_ref, sem = refs[-2:]
        copies = [
            pltpu.make_async_copy(
                w_ref.at[pl.ds(i * step, step)],
                o_ref.at[pl.ds(i * step, step)],
                sem.at[i],
            )
            for i in range(parts)
        ]
        for copy in copies:
            copy.start()
        for copy in copies:
            copy.wait()

    return pl.pallas_call(
        body,
        in_specs=[ANY] * (1 + len(after)),
        out_specs=VMEM,
        out_shape=pltpu.VMEM(w.shape, w.dtype),
        scratch_shapes=[pltpu.SemaphoreType.DMA((parts,))],
        compiler_params=pltpu.CompilerParams(vmem_limit_bytes=1 << 20),
        cost_estimate=pl.CostEstimate(
            flops=0, bytes_accessed=w.size * 2, transcendentals=0
        ),
    )(pltpu.with_memory_space_constraint(w, pltpu.HBM), *after)


def call(body, out_shape, part, arrays, kept, after, flops):
    size = sum(a.size * a.dtype.itemsize for a in arrays)
    used = 1 + len(arrays) + len(kept)

    def kernel(*refs):
        body(*refs[:used], refs[used + len(after)])

    out, *kept = pl.pallas_call(
        kernel,
        in_specs=[SMEM] + [VMEM] * (used - 1) + [ANY] * len(after),
        out_specs=[VMEM] * (1 + len(kept)),
        out_shape=[out_shape] + [pltpu.VMEM(w.shape, w.dtype) for w in kept],
        input_output_aliases={1 + len(arrays) + i: 1 + i for i in range(len(kept))},
        compiler_params=pltpu.CompilerParams(vmem_limit_bytes=4 << 20),
        cost_estimate=pl.CostEstimate(
            flops=flops, bytes_accessed=size, transcendentals=0
        ),
    )(part, *arrays, *kept, *after)
    return out, kept


def gate_up(x, weights, part, after):
    m, k = x.shape
    w = weights[0].shape[1] // 2
    tile = min(w, 256)

    def body(part_ref, x_ref, g_ref, u_ref, o_ref):
        start = part_ref[0] * w

        @pl.loop(0, w // tile)
        def _(j):
            here = pl.multiple_of(j * tile, tile)
            cols = pl.ds(pl.multiple_of(start + here, tile), tile)
            for i, ref in enumerate((g_ref, u_ref)):
                o_ref[i, :, pl.ds(here, tile)] = jnp.dot(
                    x_ref[...], ref[:, cols], preferred_element_type=F32
                )

    shape = jax.ShapeDtypeStruct((2, m, w), F32)
    return call(body, shape, part, [x], weights, after, 4 * m * k * w)


def down(mine, others, weights, part, after):
    m, w = mine.shape
    n = weights[0].shape[1]
    tile = 256

    def body(part_ref, a_ref, b_ref, d_ref, o_ref):
        first = pl.multiple_of(part_ref[0] * w, w)
        second = pl.multiple_of(w - part_ref[0] * w, w)

        @pl.loop(0, n // tile)
        def _(j):
            cols = pl.ds(pl.multiple_of(j * tile, tile), tile)
            o_ref[:, cols] = jnp.dot(
                a_ref[...], d_ref[pl.ds(first, w), cols], preferred_element_type=F32
            ) + jnp.dot(
                b_ref[...], d_ref[pl.ds(second, w), cols], preferred_element_type=F32
            )

    shape = jax.ShapeDtypeStruct((m, n), F32)
    return call(body, shape, part, [mine, others], weights, after, 4 * m * w * n)


def make_shards(n):
    ring = ring_of(n)
    half = n // 2
    to_right = [(ring[i], ring[(i + 1) % n]) for i in range(n)]
    to_left = [(ring[(i + 1) % n], ring[i]) for i in range(n)]
    swap = [(0, 1), (1, 0)]

    def right(x):
        return lax.ppermute(x, "gy", to_right)

    def left(x):
        return lax.ppermute(x, "gy", to_left)

    def other(x):
        return lax.ppermute(x, "gx", swap)

    def shards(tokens, gate_weight, up_weight, down_weight):
        rows = tokens.shape[0]
        cut = rows // 2
        core = lax.axis_index("gx").astype(jnp.int32)
        keep, give = core.reshape(1), (1 - core).reshape(1)

        a, b = tokens[:cut], tokens[cut:]
        blocks = {0: [a, b]}
        theirs, ours, hidden, partial = {}, {}, {}, {}
        last = []
        wide, back = [bring(gate_weight, []), bring(up_weight, [])], []

        def multiply(span, part):
            x = jnp.concatenate([p for d in span for p in blocks[d]], axis=0)
            out, wide[:] = gate_up(x, wide, part, last)
            last[:] = [out]
            return out

        def give_part(span):
            theirs[span] = other(multiply(span, give))

        def keep_part(span):
            ours[span] = multiply(span, keep)

        def gated(span):
            both = ours[span] + theirs[span]
            h = (jax.nn.silu(both[0]) * both[1]).astype(BF16)
            hidden[span] = h, other(h)

        def put_down(span):
            out, back[:] = down(*hidden[span], back, keep, last)
            last[:] = [out]
            at = 0
            for d in span:
                partial[d] = [
                    out[at + i * cut : at + (i + 1) * cut]
                    for i in range(len(blocks[d]))
                ]
                at += len(blocks[d]) * cut

        ra, rb, la, lb = a, b, a, b
        spans = [(0, 1)] + [(d,) for d in range(2, half + 1)]
        ra, lb = right(ra), left(lb)
        rb, la = right(rb), left(la)
        blocks[1] = [ra, rb, la, lb]
        for d in range(2, half):
            now = spans[d - 2]
            if d > 2:
                ra, lb = held(ra, last), held(lb, last)
            ra, lb = right(ra), left(lb)
            give_part(now)
            if d > 2:
                gated(spans[d - 3])
            rb, la = right(held(rb, last)), left(held(la, last))
            keep_part(now)
            blocks[d] = [ra, rb, la, lb]
        blocks[half] = [right(held(ra, last)), left(held(lb, last))]
        before, far, end = spans[-3:]
        back[:] = [bring(down_weight, last)]
        give_part(before)
        gated(spans[-4]) if len(spans) > 3 else None
        keep_part(before)
        gated(before)
        give_part(far)
        keep_part(far)
        gated(far)
        give_part(end)
        put_down(far)
        keep_part(end)
        gated(end)
        put_down(end)
        for span in spans[-3::-1]:
            put_down(span)

        l_b = left(partial[half - 1][1].astype(BF16))
        r_a = right(partial[half - 1][2].astype(BF16))
        l_a = left(partial[half][0].astype(BF16))
        r_b = right(partial[half][1].astype(BF16))
        for d in range(half - 1, 0, -1):
            if d < half - 1:
                l_b = left((partial[d][1] + l_b.astype(F32)).astype(BF16))
                r_a = right((partial[d][2] + r_a.astype(F32)).astype(BF16))
            l_a = left((partial[d][0] + l_a.astype(F32)).astype(BF16))
            r_b = right((partial[d][3] + r_b.astype(F32)).astype(BF16))
        oa = partial[0][0] + l_a.astype(F32) + r_a.astype(F32)
        ob = partial[0][1] + l_b.astype(F32) + r_b.astype(F32)
        return jnp.concatenate([oa, ob], axis=0).astype(BF16)

    return shards


def solution(mesh):
    return jax.shard_map(
        make_shards(mesh.shape["gy"]),
        mesh=mesh,
        in_specs=(P(("groups", "gy"), "gx"), P("gx", "gy"), P("gx", "gy"), P("gy", "gx")),
        out_specs=P(("groups", "gy"), "gx"),
        check_vma=False,
    )
```

```python
import jax
import jax.numpy as jnp
from jax import lax
from jax.sharding import PartitionSpec as P

F32, BF16 = jnp.float32, jnp.bfloat16


def ring_of(n):
    return list(range(0, n, 2)) + list(range(n - 1, 0, -2))


def held(x, after):
    for t in after:
        t = t[(0,) * t.ndim]
        x = jnp.where(t == t, x, t.astype(x.dtype))
    return x


def make_shards(n):
    ring = ring_of(n)
    half = n // 2
    to_right = [(ring[i], ring[(i + 1) % n]) for i in range(n)]
    to_left = [(ring[(i + 1) % n], ring[i]) for i in range(n)]
    swap = [(0, 1), (1, 0)]

    def right(x):
        return lax.ppermute(x, "gy", to_right)

    def left(x):
        return lax.ppermute(x, "gy", to_left)

    def other(x):
        return lax.ppermute(x, "gx", swap)

    def shards(tokens, gate_weight, up_weight, down_weight):
        rows = tokens.shape[0]
        cut = rows // 2
        first = lax.axis_index("gx") == 0
        last, sums, hidden, partial = [], {}, {}, {}

        def dot(x, w):
            out = jnp.dot(held(x, last), w, preferred_element_type=F32)
            last[:] = [out]
            return out

        def halves(g, u):
            w = g.shape[1] // 2
            low = jnp.stack([g[:, :w], u[:, :w]])
            high = jnp.stack([g[:, w:], u[:, w:]])
            return jnp.where(first, low, high), other(jnp.where(first, high, low))

        def multiply(d):
            x = jnp.concatenate(blocks[d], axis=0)
            sums[d] = dot(x, gate_weight), dot(x, up_weight)

        def hide(d, after):
            g, u = (held(s, after) for s in sums[d])
            mine, got = halves(g, u)
            both = mine + got
            h = (jax.nn.silu(both[0]) * both[1]).astype(BF16)
            o = other(h)
            hidden[d] = jnp.concatenate(
                [jnp.where(first, h, o), jnp.where(first, o, h)], axis=1
            )

        def put_down(d):
            out = dot(hidden[d], down_weight)
            at = 0
            partial[d] = []
            for b in blocks[d]:
                partial[d].append(out[at : at + b.shape[0]])
                at += b.shape[0]

        blocks = {0: [tokens]}
        r = l = tokens
        for d in range(1, half):
            r, l = right(r), left(l)
            blocks[d] = [r, l]
        blocks[half] = [right(r[:cut]), left(l[cut:])]
        for d in range(half + 1):
            multiply(d)
        for d in range(half + 1):
            hide(d, [sums[d + 2][0]] if d < half - 1 else blocks[half][: half - d])
        for d in (half - 1, half, *range(half - 2, -1, -1)):
            put_down(d)

        back_l, back_r = partial[half]
        l = left(back_l.astype(BF16))
        r = right(back_r.astype(BF16))
        for d in range(half - 1, 0, -1):
            pl_, pr_ = partial[d]
            if d == half - 1:
                sl = jnp.concatenate([pl_[:cut] + l.astype(F32), pl_[cut:]], axis=0)
                sr = jnp.concatenate([pr_[:cut], pr_[cut:] + r.astype(F32)], axis=0)
            else:
                sl = pl_ + l.astype(F32)
                sr = pr_ + r.astype(F32)
            l, r = left(sl.astype(BF16)), right(sr.astype(BF16))
        total = partial[0][0] + l.astype(F32) + r.astype(F32)
        return total.astype(BF16)

    return shards


def solution(mesh):
    return jax.shard_map(
        make_shards(mesh.shape["gy"]),
        mesh=mesh,
        in_specs=(P(("groups", "gy"), "gx"), P("gx", "gy"), P("gx", "gy"), P("gy", "gx")),
        out_specs=P(("groups", "gy"), "gx"),
        check_vma=False,
    )
```

```python
import jax
import jax.numpy as jnp
from jax import lax
from jax.experimental import pallas as pl
from jax.experimental.pallas import tpu as pltpu
from jax.sharding import PartitionSpec as P

F32, BF16 = jnp.float32, jnp.bfloat16
ANY = pl.BlockSpec(memory_space=pl.ANY)
VMEM = pl.BlockSpec(memory_space=pltpu.VMEM)


def ring_of(n):
    return list(range(0, n, 2)) + list(range(n - 1, 0, -2))


def in_hbm(x):
    return pltpu.with_memory_space_constraint(x, pltpu.HBM)


def params(flops, read):
    return dict(
        compiler_params=pltpu.CompilerParams(vmem_limit_bytes=24 << 20),
        cost_estimate=pl.CostEstimate(
            flops=flops, bytes_accessed=read, transcendentals=0
        ),
    )


def gate_up(x, gate_weight, up_weight, part, after):
    m, k = x.shape
    w = gate_weight.shape[1] // 2
    tile, deep = min(w, 256), k // 2
    tiles = w // tile

    def body(part_ref, x_ref, g_ref, u_ref, *refs):
        o_ref = refs[-1]
        step = pl.program_id(1)
        rows = x_ref[:, pl.ds(pl.multiple_of(step * deep, deep), deep)]
        g = jnp.dot(rows, g_ref[...], preferred_element_type=F32)
        u = jnp.dot(rows, u_ref[...], preferred_element_type=F32)

        @pl.when(step == 0)
        def _():
            o_ref[0] = g
            o_ref[1] = u

        @pl.when(step != 0)
        def _():
            o_ref[0] += g
            o_ref[1] += u

    weight = pl.BlockSpec((deep, tile), lambda j, s, part: (s, part[0] * tiles + j))
    return pl.pallas_call(
        body,
        grid_spec=pltpu.PrefetchScalarGridSpec(
            num_scalar_prefetch=1,
            grid=(tiles, 2),
            in_specs=[VMEM, weight, weight] + [ANY] * len(after),
            out_specs=pl.BlockSpec((2, m, tile), lambda j, s, part: (0, 0, j)),
        ),
        out_shape=jax.ShapeDtypeStruct((2, m, w), F32),
        **params(4 * m * k * w, 4 * k * w),
    )(part, x, in_hbm(gate_weight), in_hbm(up_weight), *after)


def down(mine, others, weight, part, cut):
    m, w = mine.shape
    n = weight.shape[1]
    tile = 512

    def body(part_ref, a_ref, b_ref, d_ref, l_ref, r_ref, o_ref, h_ref):
        @pl.when(pl.program_id(0) == 0)
        def _():
            h_ref[:, pl.ds(pl.multiple_of(part_ref[0] * w, w), w)] = a_ref[...]
            h_ref[:, pl.ds(pl.multiple_of(w - part_ref[0] * w, w), w)] = b_ref[...]

        out = jnp.dot(h_ref[...], d_ref[...], preferred_element_type=F32)
        l_ref[...] = out[:cut].astype(BF16)
        r_ref[...] = out[cut : 2 * cut].astype(BF16)
        o_ref[...] = out[2 * cut :]

    return pl.pallas_call(
        body,
        grid_spec=pltpu.PrefetchScalarGridSpec(
            num_scalar_prefetch=1,
            grid=(n // tile,),
            in_specs=[VMEM, VMEM, pl.BlockSpec((2 * w, tile), lambda j, part: (0, j))],
            out_specs=[
                pl.BlockSpec((r, tile), lambda j, part: (0, j))
                for r in (cut, cut, m - 2 * cut)
            ],
            scratch_shapes=[pltpu.VMEM((m, 2 * w), BF16)],
        ),
        out_shape=[
            jax.ShapeDtypeStruct((cut, n), BF16),
            jax.ShapeDtypeStruct((cut, n), BF16),
            jax.ShapeDtypeStruct((m - 2 * cut, n), F32),
        ],
        **params(4 * m * w * n, 4 * w * n),
    )(part, mine, others, in_hbm(weight))


def gate(*arrays, after=()):
    return pl.pallas_call(
        lambda *refs: None,
        in_specs=[ANY] * (len(arrays) + len(after)),
        out_specs=[ANY] * len(arrays),
        out_shape=[jax.ShapeDtypeStruct(x.shape, x.dtype) for x in arrays],
        input_output_aliases={i: i for i in range(len(arrays))},
        cost_estimate=pl.CostEstimate(flops=0, bytes_accessed=0, transcendentals=0),
    )(*arrays, *after)


def make_shards(n):
    ring = ring_of(n)
    half = n // 2
    to_right = [(ring[i], ring[(i + 1) % n]) for i in range(n)]
    to_left = [(ring[(i + 1) % n], ring[i]) for i in range(n)]
    swap = [(0, 1), (1, 0)]

    def right(x):
        return lax.ppermute(x, "gy", to_right)

    def left(x):
        return lax.ppermute(x, "gy", to_left)

    def other(x):
        return lax.ppermute(x, "gx", swap)

    def shards(tokens, gate_weight, up_weight, down_weight):
        rows = tokens.shape[0]
        cut = rows // 2
        core = lax.axis_index("gx").astype(jnp.int32)
        keep, give = core.reshape(1), (1 - core).reshape(1)
        a, b = tokens[:cut], tokens[cut:]

        def kernels(x, after):
            theirs = gate_up(x, gate_weight, up_weight, give, after)
            (theirs,) = yield [theirs]
            got = other(theirs)
            ours = gate_up(x, gate_weight, up_weight, keep, [theirs])
            ours, got = yield [ours, got]
            h = (jax.nn.silu(ours[0] + got[0]) * (ours[1] + got[1])).astype(BF16)
            yield down(h, other(h), down_weight, keep, cut)

        def gather(r, l, hops):
            found = []
            for _ in range(hops):
                r, l = right(r), left(l)
                found = [r, l] + found
            return found

        def stack(pieces):
            return jnp.concatenate(pieces, axis=0)

        def add(part, block):
            return (part + block.astype(F32)).astype(BF16)

        early = gather(a, b, half - 1)
        early[0], early[1], r, l = gate(early[0], early[1], b, a)
        far = gather(early[0], early[1], 1) + early
        steps = kernels(stack(far), [])
        near, step = [], next(steps)
        for hop in range(half - 1):
            r, l = right(r), left(l)
            if hop < 2:
                r, l, *back = gate(r, l, *step)
                step = steps.send(back)
            elif hop < half - 2:
                r, l = gate(r, l)
            near = [r, l] + near
        l, r, sums = step

        steps = kernels(stack(near + [a, b]), [sums])
        step = next(steps)
        l, r = left(l), right(r)
        for hop in range(half - 1):
            if hop < 2:
                l, r, *back = gate(l, r, *step)
                step = steps.send(back)
            else:
                l, r = gate(l, r, after=step if hop == 2 else ())
            i = 2 * hop * cut
            l = left(add(sums[i : i + cut], l))
            r = right(add(sums[i + cut : i + 2 * cut], r))
        far_a, far_b = l, r
        l, r, sums = step
        l, r = left(l), right(r)
        for hop in range(half - 2):
            if hop == 0:
                l, r, far_a, far_b = gate(l, r, far_a, far_b)
            else:
                l, r = gate(l, r)
            i = 2 * hop * cut
            l = left(add(sums[i : i + cut], l))
            r = right(add(sums[i + cut : i + 2 * cut], r))
        l, r = gate(l, r)
        total_a = sums[-2 * cut : -cut] + far_a.astype(F32) + r.astype(F32)
        total_b = sums[-cut:] + far_b.astype(F32) + l.astype(F32)
        return jnp.concatenate([total_a, total_b], axis=0).astype(BF16)

    return shards


def solution(mesh):
    return jax.shard_map(
        make_shards(mesh.shape["gy"]),
        mesh=mesh,
        in_specs=(P(("groups", "gy"), "gx"), P("gx", "gy"), P("gx", "gy"), P("gy", "gx")),
        out_specs=P(("groups", "gy"), "gx"),
        check_vma=False,
    )
```

```python
import jax
import jax.numpy as jnp
from jax import lax
from jax.experimental import pallas as pl
from jax.experimental.pallas import tpu as pltpu
from jax.sharding import PartitionSpec as P

F32, BF16 = jnp.float32, jnp.bfloat16
ANY = pl.BlockSpec(memory_space=pl.ANY)
VMEM = pl.BlockSpec(memory_space=pltpu.VMEM)


def ring_of(n):
    return list(range(0, n, 2)) + list(range(n - 1, 0, -2))


def in_hbm(x):
    return pltpu.with_memory_space_constraint(x, pltpu.HBM)


def params(flops, read):
    return dict(
        compiler_params=pltpu.CompilerParams(vmem_limit_bytes=16 << 20),
        cost_estimate=pl.CostEstimate(
            flops=flops, bytes_accessed=read, transcendentals=0
        ),
    )


def gate_up(x, gate_weight, up_weight, part, after):
    m, k = x.shape
    w = gate_weight.shape[1] // 2
    deep = 512

    def body(part_ref, x_ref, g_ref, u_ref, *refs):
        o_ref = refs[-1]
        step = pl.program_id(0)

        @pl.when(step == 0)
        def _():
            o_ref[...] = jnp.zeros_like(o_ref)

        cols = pl.ds(pl.multiple_of(step * deep, deep), deep)
        o_ref[0] += jnp.dot(x_ref[:, cols], g_ref[...], preferred_element_type=F32)
        o_ref[1] += jnp.dot(x_ref[:, cols], u_ref[...], preferred_element_type=F32)

    weight = pl.BlockSpec((deep, w), lambda s, part: (s, part[0]))
    return pl.pallas_call(
        body,
        grid_spec=pltpu.PrefetchScalarGridSpec(
            num_scalar_prefetch=1,
            grid=(k // deep,),
            in_specs=[VMEM, weight, weight] + [ANY] * len(after),
            out_specs=VMEM,
        ),
        out_shape=jax.ShapeDtypeStruct((2, m, w), F32),
        **params(4 * m * k * w, 4 * k * w),
    )(part, x, in_hbm(gate_weight), in_hbm(up_weight), *after)


def down(mine, others, weight, part, cut):
    m, w = mine.shape
    n = weight.shape[1]
    tile, deep = n // 2, min(2 * w, 512)
    steps = 2 * w // deep

    def body(part_ref, a_ref, b_ref, d_ref, l_ref, r_ref, o_ref, h_ref, s_ref):
        j, step = pl.program_id(0), pl.program_id(1)

        @pl.when((j == 0) & (step == 0))
        def _():
            h_ref[:, pl.ds(pl.multiple_of(part_ref[0] * w, w), w)] = a_ref[...]
            h_ref[:, pl.ds(pl.multiple_of(w - part_ref[0] * w, w), w)] = b_ref[...]

        @pl.when(step == 0)
        def _():
            s_ref[...] = jnp.zeros_like(s_ref)

        rows = h_ref[:, pl.ds(pl.multiple_of(step * deep, deep), deep)]
        s_ref[...] += jnp.dot(rows, d_ref[...], preferred_element_type=F32)

        @pl.when(step == steps - 1)
        def _():
            cols = pl.ds(pl.multiple_of(j * tile, tile), tile)
            l_ref[:, cols] = s_ref[:cut].astype(BF16)
            r_ref[:, cols] = s_ref[cut : 2 * cut].astype(BF16)
            o_ref[:, cols] = s_ref[2 * cut :]

    return pl.pallas_call(
        body,
        grid_spec=pltpu.PrefetchScalarGridSpec(
            num_scalar_prefetch=1,
            grid=(2, steps),
            in_specs=[
                VMEM,
                VMEM,
                pl.BlockSpec((deep, tile), lambda j, s, part: (s, j)),
            ],
            out_specs=[VMEM, VMEM, VMEM],
            scratch_shapes=[pltpu.VMEM((m, 2 * w), BF16), pltpu.VMEM((m, tile), F32)],
        ),
        out_shape=[
            jax.ShapeDtypeStruct((cut, n), BF16),
            jax.ShapeDtypeStruct((cut, n), BF16),
            jax.ShapeDtypeStruct((m - 2 * cut, n), F32),
        ],
        **params(4 * m * w * n, 4 * w * n),
    )(part, mine, others, in_hbm(weight))


def gate(*arrays, after=()):
    return pl.pallas_call(
        lambda *refs: None,
        in_specs=[ANY] * (len(arrays) + len(after)),
        out_specs=[ANY] * len(arrays),
        out_shape=[jax.ShapeDtypeStruct(x.shape, x.dtype) for x in arrays],
        input_output_aliases={i: i for i in range(len(arrays))},
        compiler_params=pltpu.CompilerParams(vmem_limit_bytes=1 << 18),
        cost_estimate=pl.CostEstimate(flops=0, bytes_accessed=0, transcendentals=0),
    )(*arrays, *after)


def make_shards(n):
    ring = ring_of(n)
    half = n // 2
    to_right = [(ring[i], ring[(i + 1) % n]) for i in range(n)]
    to_left = [(ring[(i + 1) % n], ring[i]) for i in range(n)]
    swap = [(0, 1), (1, 0)]

    def right(x):
        return lax.ppermute(x, "gy", to_right)

    def left(x):
        return lax.ppermute(x, "gy", to_left)

    def other(x):
        return lax.ppermute(x, "gx", swap)

    def shards(tokens, gate_weight, up_weight, down_weight):
        rows = tokens.shape[0]
        cut = rows // 2
        core = lax.axis_index("gx").astype(jnp.int32)
        keep, give = core.reshape(1), (1 - core).reshape(1)
        a, b = tokens[:cut], tokens[cut:]

        def kernels(x, after):
            theirs = gate_up(x, gate_weight, up_weight, give, after)
            (theirs,) = yield [theirs]
            got = other(theirs)
            ours = gate_up(x, gate_weight, up_weight, keep, [theirs])
            ours, got = yield [ours, got]
            h = (jax.nn.silu(ours[0] + got[0]) * (ours[1] + got[1])).astype(BF16)
            yield down(h, other(h), down_weight, keep, cut)

        def gather(r, l, hops):
            found = []
            for _ in range(hops):
                r, l = right(r), left(l)
                found = [r, l] + found
            return found

        def stack(pieces):
            return jnp.concatenate(pieces, axis=0)

        def add(part, block):
            return (part + block.astype(F32)).astype(BF16)

        early = gather(a, b, half - 1)
        early[0], early[1] = gate(early[0], early[1])
        r, l = gate(b, a, after=early[:2])
        far = gather(early[0], early[1], 1) + early
        steps = kernels(stack(far), [])
        near, step = [], next(steps)
        for hop in range(half - 1):
            r, l = right(r), left(l)
            if hop < 2:
                r, l, *back = gate(r, l, *step)
                step = steps.send(back)
            elif hop < half - 2:
                r, l = gate(r, l)
            near = [r, l] + near
        l, r, sums = step

        steps = kernels(stack(near + [a, b]), [sums])
        step = next(steps)
        l, r = left(l), right(r)
        for hop in range(half - 1):
            if hop < 2:
                l, r, *back = gate(l, r, *step)
                step = steps.send(back)
            else:
                l, r = gate(l, r, after=step if hop == 2 else ())
            i = 2 * hop * cut
            l = left(add(sums[i : i + cut], l))
            r = right(add(sums[i + cut : i + 2 * cut], r))
        far_a, far_b = l, r
        l, r, sums = step
        l, r = left(l), right(r)
        for hop in range(half - 2):
            if hop == 0:
                l, r, far_a, far_b = gate(l, r, far_a, far_b)
            else:
                l, r = gate(l, r)
            i = 2 * hop * cut
            l = left(add(sums[i : i + cut], l))
            r = right(add(sums[i + cut : i + 2 * cut], r))
        l, r = gate(l, r)
        total_a = sums[-2 * cut : -cut] + far_a.astype(F32) + r.astype(F32)
        total_b = sums[-cut:] + far_b.astype(F32) + l.astype(F32)
        return jnp.concatenate([total_a, total_b], axis=0).astype(BF16)

    return shards


def solution(mesh):
    return jax.shard_map(
        make_shards(mesh.shape["gy"]),
        mesh=mesh,
        in_specs=(P(("groups", "gy"), "gx"), P("gx", "gy"), P("gx", "gy"), P("gy", "gx")),
        out_specs=P(("groups", "gy"), "gx"),
        check_vma=False,
    )
```

```python
import jax
import jax.numpy as jnp
from jax import lax
from jax.experimental import pallas as pl
from jax.experimental.pallas import tpu as pltpu
from jax.sharding import PartitionSpec as P

F32, BF16 = jnp.float32, jnp.bfloat16
ANY = pl.BlockSpec(memory_space=pl.ANY)
SMEM = pl.BlockSpec(memory_space=pltpu.SMEM)
VMEM = pl.BlockSpec(memory_space=pltpu.VMEM)


def ring_of(n):
    return list(range(0, n, 2)) + list(range(n - 1, 0, -2))


def in_hbm(x):
    return pltpu.with_memory_space_constraint(x, pltpu.HBM)


def params(flops, read):
    return dict(
        compiler_params=pltpu.CompilerParams(vmem_limit_bytes=24 << 20),
        cost_estimate=pl.CostEstimate(
            flops=flops, bytes_accessed=read, transcendentals=0
        ),
    )


def gate_up(x, gate_weight, up_weight, part, after):
    m, k = x.shape
    w = gate_weight.shape[1] // 2
    deep = 512
    steps = k // deep

    def body(part_ref, x_ref, *refs):
        weights, (o_ref, held_ref, sems) = refs[:2], refs[-3:]
        cols = pl.ds(pl.multiple_of(part_ref[0] * w, w), w)

        def fetch(i, s):
            rows = pl.ds(pl.multiple_of(s * deep, deep), deep)
            return pltpu.make_async_copy(
                weights[i].at[rows, cols], held_ref.at[i, s], sems.at[i, s]
            )

        for s in range(steps):
            for i in range(2):
                fetch(i, s).start()
        o_ref[...] = jnp.zeros_like(o_ref)

        @pl.loop(0, steps)
        def _(s):
            here = pl.ds(pl.multiple_of(s * deep, deep), deep)
            for i in range(2):
                fetch(i, s).wait()
                o_ref[i] += jnp.dot(
                    x_ref[:, here], held_ref[i, s], preferred_element_type=F32
                )

    return pl.pallas_call(
        body,
        in_specs=[SMEM, VMEM] + [ANY] * (2 + len(after)),
        out_specs=VMEM,
        out_shape=jax.ShapeDtypeStruct((2, m, w), F32),
        scratch_shapes=[
            pltpu.VMEM((2, steps, deep, w), BF16),
            pltpu.SemaphoreType.DMA((2, steps)),
        ],
        **params(4 * m * k * w, 4 * k * w),
    )(part, x, in_hbm(gate_weight), in_hbm(up_weight), *after)


def down(mine, others, weight, part, cut):
    m, w = mine.shape
    n = weight.shape[1]
    tile = 512
    steps = n // tile

    def body(part_ref, a_ref, b_ref, d_ref, l_ref, r_ref, o_ref, h_ref, held_ref, sems):
        def fetch(j):
            cols = pl.ds(pl.multiple_of(j * tile, tile), tile)
            return pltpu.make_async_copy(d_ref.at[:, cols], held_ref.at[j], sems.at[j])

        for j in range(steps):
            fetch(j).start()
        h_ref[:, pl.ds(pl.multiple_of(part_ref[0] * w, w), w)] = a_ref[...]
        h_ref[:, pl.ds(pl.multiple_of(w - part_ref[0] * w, w), w)] = b_ref[...]

        @pl.loop(0, steps)
        def _(j):
            cols = pl.ds(pl.multiple_of(j * tile, tile), tile)
            fetch(j).wait()
            out = jnp.dot(h_ref[...], held_ref[j], preferred_element_type=F32)
            l_ref[:, cols] = out[:cut].astype(BF16)
            r_ref[:, cols] = out[cut : 2 * cut].astype(BF16)
            o_ref[:, cols] = out[2 * cut :]

    return pl.pallas_call(
        body,
        in_specs=[SMEM, VMEM, VMEM, ANY],
        out_specs=[VMEM] * 3,
        out_shape=[
            jax.ShapeDtypeStruct((cut, n), BF16),
            jax.ShapeDtypeStruct((cut, n), BF16),
            jax.ShapeDtypeStruct((m - 2 * cut, n), F32),
        ],
        scratch_shapes=[
            pltpu.VMEM((m, 2 * w), BF16),
            pltpu.VMEM((steps, 2 * w, tile), BF16),
            pltpu.SemaphoreType.DMA((steps,)),
        ],
        **params(4 * m * w * n, 4 * w * n),
    )(part, mine, others, in_hbm(weight))


def gate(*arrays, after=()):
    return pl.pallas_call(
        lambda *refs: None,
        in_specs=[ANY] * (len(arrays) + len(after)),
        out_specs=[ANY] * len(arrays),
        out_shape=[jax.ShapeDtypeStruct(x.shape, x.dtype) for x in arrays],
        input_output_aliases={i: i for i in range(len(arrays))},
        compiler_params=pltpu.CompilerParams(vmem_limit_bytes=1 << 18),
        cost_estimate=pl.CostEstimate(flops=0, bytes_accessed=0, transcendentals=0),
    )(*arrays, *after)


def make_shards(n):
    ring = ring_of(n)
    half = n // 2
    to_right = [(ring[i], ring[(i + 1) % n]) for i in range(n)]
    to_left = [(ring[(i + 1) % n], ring[i]) for i in range(n)]
    swap = [(0, 1), (1, 0)]

    def right(x):
        return lax.ppermute(x, "gy", to_right)

    def left(x):
        return lax.ppermute(x, "gy", to_left)

    def other(x):
        return lax.ppermute(x, "gx", swap)

    def shards(tokens, gate_weight, up_weight, down_weight):
        rows = tokens.shape[0]
        cut = rows // 2
        core = lax.axis_index("gx").astype(jnp.int32)
        keep, give = core.reshape(1), (1 - core).reshape(1)
        a, b = tokens[:cut], tokens[cut:]

        def kernels(x, after):
            theirs = gate_up(x, gate_weight, up_weight, give, after)
            (theirs,) = yield [theirs]
            got = other(theirs)
            ours = gate_up(x, gate_weight, up_weight, keep, [theirs])
            ours, got = yield [ours, got]
            h = (jax.nn.silu(ours[0] + got[0]) * (ours[1] + got[1])).astype(BF16)
            yield down(h, other(h), down_weight, keep, cut)

        def gather(r, l, hops):
            found = []
            for _ in range(hops):
                r, l = right(r), left(l)
                found = [r, l] + found
            return found

        def stack(pieces):
            return jnp.concatenate(pieces, axis=0)

        def add(part, block):
            return (part + block.astype(F32)).astype(BF16)

        early = gather(a, b, half - 1)
        early[0], early[1] = gate(early[0], early[1])
        r, l = gate(b, a, after=early[:2])
        far = gather(early[0], early[1], 1) + early
        steps = kernels(stack(far), [])
        near, step = [], next(steps)
        for hop in range(half - 1):
            r, l = right(r), left(l)
            if hop < 2:
                r, l, *back = gate(r, l, *step)
                step = steps.send(back)
            elif hop < half - 2:
                r, l = gate(r, l)
            near = [r, l] + near
        l, r, sums = step

        steps = kernels(stack(near + [a, b]), [sums])
        step = next(steps)
        l, r = left(l), right(r)
        for hop in range(half - 1):
            if hop < 2:
                l, r, *back = gate(l, r, *step)
                step = steps.send(back)
            else:
                l, r = gate(l, r, after=step if hop == 2 else ())
            i = 2 * hop * cut
            l = left(add(sums[i : i + cut], l))
            r = right(add(sums[i + cut : i + 2 * cut], r))
        far_a, far_b = l, r
        l, r, sums = step
        l, r = left(l), right(r)
        for hop in range(half - 2):
            if hop == 0:
                l, r, far_a, far_b = gate(l, r, far_a, far_b)
            else:
                l, r = gate(l, r)
            i = 2 * hop * cut
            l = left(add(sums[i : i + cut], l))
            r = right(add(sums[i + cut : i + 2 * cut], r))
        l, r = gate(l, r)
        total_a = sums[-2 * cut : -cut] + far_a.astype(F32) + r.astype(F32)
        total_b = sums[-cut:] + far_b.astype(F32) + l.astype(F32)
        return jnp.concatenate([total_a, total_b], axis=0).astype(BF16)

    return shards


def solution(mesh):
    return jax.shard_map(
        make_shards(mesh.shape["gy"]),
        mesh=mesh,
        in_specs=(P(("groups", "gy"), "gx"), P("gx", "gy"), P("gx", "gy"), P("gy", "gx")),
        out_specs=P(("groups", "gy"), "gx"),
        check_vma=False,
    )
```

```python
import jax
import jax.numpy as jnp
from jax import lax
from jax.experimental import pallas as pl
from jax.experimental.pallas import tpu as pltpu
from jax.sharding import PartitionSpec as P

F32, BF16 = jnp.float32, jnp.bfloat16
ANY = pl.BlockSpec(memory_space=pl.ANY)
SMEM = pl.BlockSpec(memory_space=pltpu.SMEM)
VMEM = pl.BlockSpec(memory_space=pltpu.VMEM)


def ring_of(n):
    return list(range(0, n, 2)) + list(range(n - 1, 0, -2))


def in_hbm(x):
    return pltpu.with_memory_space_constraint(x, pltpu.HBM)


def in_vmem(x):
    return pltpu.with_memory_space_constraint(x, pltpu.VMEM)


def params(vmem, flops, read):
    return dict(
        compiler_params=pltpu.CompilerParams(vmem_limit_bytes=vmem),
        cost_estimate=pl.CostEstimate(
            flops=flops, bytes_accessed=read, transcendentals=0
        ),
    )


def gate(*arrays, after=()):
    return pl.pallas_call(
        lambda *refs: None,
        in_specs=[ANY] * (len(arrays) + len(after)),
        out_specs=[ANY] * len(arrays),
        out_shape=[jax.ShapeDtypeStruct(x.shape, x.dtype) for x in arrays],
        input_output_aliases={i: i for i in range(len(arrays))},
        **params(1 << 18, 0, 0),
    )(*arrays, *after)


def split(r, l):
    cut, n = r.shape[0] // 2, r.shape[1]
    if cut % 16:
        return r[:cut], l[cut:]

    def body(r_ref, l_ref, a_ref, b_ref):
        a_ref[...] = r_ref[:cut]
        b_ref[...] = l_ref[cut:]

    return pl.pallas_call(
        body,
        in_specs=[VMEM, VMEM],
        out_specs=[VMEM, VMEM],
        out_shape=[jax.ShapeDtypeStruct((cut, n), r.dtype)] * 2,
        **params(4 << 20, 0, 8 * cut * n),
    )(r, l)


def bring(weights, parts, after, pieces=8):
    k, w = weights[0].shape[0], weights[0].shape[1] // 2
    step = k // pieces
    count = len(weights) * len(parts)

    def body(*refs):
        sources, refs = refs[: len(weights)], refs[len(weights) :]
        targets, sems = refs[-1 - count : -1], refs[-1]
        copies = []
        for i, target in enumerate(targets):
            start = pl.multiple_of(refs[i // len(weights)][0] * w, w)
            for s in range(pieces):
                rows = pl.ds(s * step, step)
                copies.append(
                    pltpu.make_async_copy(
                        sources[i % len(weights)].at[rows, pl.ds(start, w)],
                        target.at[rows],
                        sems.at[i, s],
                    )
                )
        for copy in copies:
            copy.start()
        for copy in copies:
            copy.wait()

    return pl.pallas_call(
        body,
        in_specs=[ANY] * len(weights) + [SMEM] * len(parts) + [ANY] * len(after),
        out_specs=[VMEM] * count,
        out_shape=[pltpu.VMEM((k, w), weights[0].dtype)] * count,
        scratch_shapes=[pltpu.SemaphoreType.DMA((count, pieces))],
        **params(1 << 18, 0, 4 * sum(w.size for w in weights)),
    )(*map(in_hbm, weights), *parts, *after)


def gate_up(pieces, weights, after):
    if any(p.shape[0] % 16 for p in pieces):
        pieces = [jnp.concatenate(pieces, axis=0)]
    m, k = sum(p.shape[0] for p in pieces), pieces[0].shape[1]
    w = weights[0].shape[1]
    tile = min(w, 256)
    count, halves = len(pieces), len(weights) // 2

    def body(*refs):
        weight_refs = refs[count : count + len(weights)]
        out_refs, x_ref = refs[-1 - halves : -1], refs[-1]
        at = 0
        for ref in refs[:count]:
            x_ref[at : at + ref.shape[0]] = ref[...]
            at += ref.shape[0]

        @pl.loop(0, w // tile)
        def _(j):
            cols = pl.ds(pl.multiple_of(j * tile, tile), tile)
            for i, ref in enumerate(weight_refs):
                out_refs[i // 2][i % 2, :, cols] = jnp.dot(
                    x_ref[...], ref[:, cols], preferred_element_type=F32
                )

    shape = jax.ShapeDtypeStruct((2, m, w), F32)
    return pl.pallas_call(
        body,
        in_specs=[VMEM] * (count + len(weights)) + [ANY] * len(after),
        out_specs=[VMEM] * halves,
        out_shape=[shape] * halves,
        scratch_shapes=[pltpu.VMEM((m, k), BF16)],
        **params(6 << 20, 4 * halves * m * k * w, 4 * halves * k * w),
    )(*pieces, *map(in_vmem, weights), *after)


def gated(ours, theirs):
    _, m, w = ours.shape
    tile = min(w, 256)

    def body(a_ref, b_ref, o_ref):
        @pl.loop(0, w // tile)
        def _(j):
            cols = pl.ds(pl.multiple_of(j * tile, tile), tile)
            v = a_ref[0, :, cols] + b_ref[0, :, cols]
            u = a_ref[1, :, cols] + b_ref[1, :, cols]
            o_ref[:, cols] = (v / (1.0 + jnp.exp(-v)) * u).astype(BF16)

    return pl.pallas_call(
        body,
        in_specs=[VMEM, VMEM],
        out_specs=VMEM,
        out_shape=jax.ShapeDtypeStruct((m, w), BF16),
        **params(4 << 20, 8 * m * w, 16 * m * w),
    )(ours, theirs)


def down(halves, weight, part, outs, after):
    m = sum(h.shape[0] for h, _ in halves)
    w = halves[0][0].shape[1]
    n = weight.shape[1]
    tile, deep = 512, min(2 * w, 512)
    steps = n // tile
    if any(h.shape[0] % 16 for h, _ in halves):
        halves = [tuple(jnp.concatenate(hs, axis=0) for hs in zip(*halves))]
    count = len(halves)

    def body(part_ref, *refs):
        d_ref, (h_ref, held_ref, sems) = refs[2 * count], refs[-3:]
        out_refs = refs[-3 - len(outs) : -3]

        def fetch(j, i):
            rows = pl.ds(i * deep, deep)
            cols = pl.ds(pl.multiple_of(j * tile, tile), tile)
            return pltpu.make_async_copy(
                d_ref.at[rows, cols], held_ref.at[j, rows], sems.at[j, i]
            )

        for j in range(steps):
            for i in range(2 * w // deep):
                fetch(j, i).start()
        at = 0
        for i in range(count):
            rows = slice(at, at + refs[2 * i].shape[0])
            at = rows.stop
            first = pl.multiple_of(part_ref[0] * w, w)
            h_ref[rows, pl.ds(first, w)] = refs[2 * i][...]
            h_ref[rows, pl.ds(pl.multiple_of(w - first, w), w)] = refs[2 * i + 1][...]

        @pl.loop(0, steps)
        def _(j):
            cols = pl.ds(pl.multiple_of(j * tile, tile), tile)
            for i in range(2 * w // deep):
                fetch(j, i).wait()
            out = jnp.dot(h_ref[...], held_ref[j], preferred_element_type=F32)
            for (at, size, dtype), ref in zip(outs, out_refs):
                ref[:, cols] = out[at : at + size].astype(dtype)

    return pl.pallas_call(
        body,
        in_specs=[SMEM] + [VMEM] * (2 * count) + [ANY] * (1 + len(after)),
        out_specs=[VMEM] * len(outs),
        out_shape=[jax.ShapeDtypeStruct((size, n), dtype) for _, size, dtype in outs],
        scratch_shapes=[
            pltpu.VMEM((m, 2 * w), BF16),
            pltpu.VMEM((steps, 2 * w, tile), BF16),
            pltpu.SemaphoreType.DMA((steps, 2 * w // deep)),
        ],
        **params(24 << 20, 4 * m * w * n, 4 * w * n),
    )(part, *[h for pair in halves for h in pair], in_hbm(weight), *after)


def make_shards(n):
    ring = ring_of(n)
    half = n // 2
    to_right = [(ring[i], ring[(i + 1) % n]) for i in range(n)]
    to_left = [(ring[(i + 1) % n], ring[i]) for i in range(n)]
    swap = [(0, 1), (1, 0)]

    def right(x):
        return lax.ppermute(x, "gy", to_right)

    def left(x):
        return lax.ppermute(x, "gy", to_left)

    def other(x):
        return lax.ppermute(x, "gx", swap)

    def add(part, block):
        return (part + block.astype(F32)).astype(BF16)

    def shards(tokens, gate_weight, up_weight, down_weight):
        rows = tokens.shape[0]
        cut = rows // 2
        core = lax.axis_index("gx").astype(jnp.int32)
        keep, give = core.reshape(1), (1 - core).reshape(1)

        r, l = right(tokens), left(tokens)
        wide = bring([gate_weight, up_weight], [give, keep], [])
        r, l = gate(r, l, after=wide[-1:])
        groups, sums = [[tokens, r, l]], []
        for d in range(2, half):
            r, l = right(r), left(l)
            theirs, ours = gate_up(groups[-1], wide, sums[-1:])
            r, l, theirs, ours = gate(r, l, theirs, ours)
            groups.append([r, l])
            sums += [theirs, ours]
        far_l, far_r = split(r, l)
        far_l, far_r = right(far_l), left(far_r)
        got = [other(theirs) for theirs in sums[::2]]
        far_l, far_r, r, l, *got = gate(far_l, far_r, r, l, *got)

        def hide(ours, got):
            h = gated(ours, got)
            return h, other(h)

        (theirs,) = gate_up([far_l, far_r, r, l], wide[:2], [])
        far_got = other(theirs)
        (ours,) = gate_up([far_l, far_r, r, l], wide[2:], [theirs])
        far = hide(ours, far_got)
        near = [hide(*pair) for pair in zip(sums[1::2], got)]
        at = [(i * cut, cut) for i in range(6)]
        outs = [(*at[3], BF16), (*at[4], BF16), (*at[0], BF16), (*at[1], BF16)]
        outs += [(*at[2], F32), (*at[5], F32)]
        b_l, b_r, a_l, a_r, next_l, next_r = down([far], down_weight, keep, outs, [])

        b_l, b_r = left(b_l), right(b_r)
        a_l, a_r = left(a_l), right(a_r)
        size = rows * (2 * half - 3)
        (rest,) = down(near, down_weight, keep, [(0, size, F32)], [next_l])

        def parts(d):
            first = rows * (2 * d - 1)
            return [rest[first + i * cut : first + (i + 1) * cut] for i in range(4)]

        after = [rest]
        for d in range(half - 2, -1, -1):
            b_l, b_r = gate(b_l, b_r, after=after)
            if d > 0:
                _, left_b, right_a, _ = parts(d)
                b_l, b_r = add(left_b, b_l), add(right_a, b_r)
                after = [b_l, b_r]
                b_l, b_r = left(b_l), right(b_r)
            else:
                after = [b_l, b_r]
            a_l, a_r = gate(a_l, a_r, after=after)
            a_l, a_r = add(next_l, a_l), add(next_r, a_r)
            after = [a_l, a_r]
            a_l, a_r = left(a_l), right(a_r)
            if d > 0:
                next_l, _, _, next_r = parts(d)
        a_l, a_r = gate(a_l, a_r)
        total_a = rest[:cut] + a_l.astype(F32) + b_r.astype(F32)
        total_b = rest[cut:rows] + a_r.astype(F32) + b_l.astype(F32)
        return jnp.concatenate([total_a, total_b], axis=0).astype(BF16)

    return shards


def solution(mesh):
    return jax.shard_map(
        make_shards(mesh.shape["gy"]),
        mesh=mesh,
        in_specs=(P(("groups", "gy"), "gx"), P("gx", "gy"), P("gx", "gy"), P("gy", "gx")),
        out_specs=P(("groups", "gy"), "gx"),
        check_vma=False,
    )
```

```python
import jax
import jax.numpy as jnp
from jax import lax
from jax.experimental import pallas as pl
from jax.experimental.pallas import tpu as pltpu
from jax.sharding import PartitionSpec as P

F32, BF16 = jnp.float32, jnp.bfloat16
ANY = pl.BlockSpec(memory_space=pl.ANY)
SMEM = pl.BlockSpec(memory_space=pltpu.SMEM)
VMEM = pl.BlockSpec(memory_space=pltpu.VMEM)


def ring_of(n):
    return list(range(0, n, 2)) + list(range(n - 1, 0, -2))


def in_hbm(x):
    return pltpu.with_memory_space_constraint(x, pltpu.HBM)


def in_vmem(x):
    return pltpu.with_memory_space_constraint(x, pltpu.VMEM)


GATE, KERNEL = 22_000_000_000, 5_500_000_000


def params(vmem, work=0):
    return dict(
        compiler_params=pltpu.CompilerParams(vmem_limit_bytes=vmem),
        cost_estimate=pl.CostEstimate(flops=work, bytes_accessed=0, transcendentals=0),
    )


def gate(*arrays, after=(), work=0):
    return pl.pallas_call(
        lambda *refs: None,
        name="gate",
        in_specs=[ANY] * (len(arrays) + len(after)),
        out_specs=[ANY] * len(arrays),
        out_shape=[jax.ShapeDtypeStruct(x.shape, x.dtype) for x in arrays],
        input_output_aliases={i: i for i in range(len(arrays))},
        **params(1 << 18, work),
    )(*arrays, *after)


def fetches(sources, targets, sems, pieces=8):
    copies = []
    for i, ((source, start), target) in enumerate(zip(sources, targets)):
        step = target.shape[0] // pieces
        for s in range(pieces):
            rows = pl.ds(s * step, step)
            cols = pl.ds(start, target.shape[1])
            copies.append(
                pltpu.make_async_copy(
                    source.at[rows, cols], target.at[rows], sems.at[i, s]
                )
            )
    return copies


def bring(weights, part, after):
    k, w = weights[0].shape[0], weights[0].shape[1] // 2
    count = len(weights)

    def body(part_ref, *refs):
        start = pl.multiple_of(part_ref[0] * w, w)
        sources = [(ref, start) for ref in refs[:count]]
        copies = fetches(sources, refs[-1 - count : -1], refs[-1])
        for copy in copies:
            copy.start()
        for copy in copies:
            copy.wait()

    return pl.pallas_call(
        body,
        name="bring",
        in_specs=[SMEM] + [ANY] * (count + len(after)),
        out_specs=[VMEM] * count,
        out_shape=[pltpu.VMEM((k, w), weights[0].dtype)] * count,
        scratch_shapes=[pltpu.SemaphoreType.DMA((count, 8))],
        **params(1 << 18, KERNEL),
    )(part, *map(in_hbm, weights), *after)


def gate_up(pieces, weights, after, load=None):
    if any(p.shape[0] % 16 for p in pieces):
        pieces = [jnp.concatenate(pieces, axis=0)]
    m, k = sum(p.shape[0] for p in pieces), pieces[0].shape[1]
    w = weights[0].shape[1]
    tile = min(w, 256)
    count, halves = len(pieces), len(weights) // 2
    shapes = [jax.ShapeDtypeStruct((2, m, w), F32)] * halves
    scratch = [pltpu.VMEM((m, k), BF16)]
    extra = []
    if load is not None:
        wide = load.shape[1] // 2
        extra = [in_hbm(load)]
        shapes += [pltpu.VMEM((load.shape[0], wide), load.dtype)] * 2
        scratch += [pltpu.SemaphoreType.DMA((2, 8))]

    def body(*refs):
        weight_refs = refs[count : count + len(weights)]
        outs = refs[-len(shapes) - len(scratch) : -len(scratch)]
        out_refs, x_ref = outs[:halves], refs[-len(scratch)]
        copies = []
        if load is not None:
            source = refs[count + len(weights)]
            copies = fetches([(source, 0), (source, wide)], outs[halves:], refs[-1])
        for copy in copies:
            copy.start()
        at = 0
        for ref in refs[:count]:
            x_ref[at : at + ref.shape[0]] = ref[...]
            at += ref.shape[0]

        @pl.loop(0, w // tile)
        def _(j):
            cols = pl.ds(pl.multiple_of(j * tile, tile), tile)
            for i, ref in enumerate(weight_refs):
                out_refs[i // 2][i % 2, :, cols] = jnp.dot(
                    x_ref[...], ref[:, cols], preferred_element_type=F32
                )

        for copy in copies:
            copy.wait()

    return pl.pallas_call(
        body,
        name="gate_up",
        in_specs=[VMEM] * (count + len(weights)) + [ANY] * (len(extra) + len(after)),
        out_specs=[VMEM] * len(shapes),
        out_shape=shapes,
        scratch_shapes=scratch,
        **params(6 << 20, KERNEL),
    )(*pieces, *map(in_vmem, weights), *extra, *after)


def gated(ours, theirs):
    _, m, w = ours.shape
    tile = min(w, 256)

    def body(a_ref, b_ref, o_ref):
        @pl.loop(0, w // tile)
        def _(j):
            cols = pl.ds(pl.multiple_of(j * tile, tile), tile)
            v = a_ref[0, :, cols] + b_ref[0, :, cols]
            u = a_ref[1, :, cols] + b_ref[1, :, cols]
            o_ref[:, cols] = (v / (1.0 + jnp.exp(-v)) * u).astype(BF16)

    return pl.pallas_call(
        body,
        name="gated",
        in_specs=[VMEM, VMEM],
        out_specs=VMEM,
        out_shape=jax.ShapeDtypeStruct((m, w), BF16),
        **params(4 << 20),
    )(ours, theirs)


def down(halves, weights, part, outs, after):
    m = sum(h.shape[0] for h, _ in halves)
    w = halves[0][0].shape[1]
    n = weights[0].shape[1]
    tile = 512
    if any(h.shape[0] % 16 for h, _ in halves):
        halves = [tuple(jnp.concatenate(hs, axis=0) for hs in zip(*halves))]
    count = len(halves)

    def body(part_ref, *refs):
        weight_refs, h_ref = refs[2 * count : 2 * count + 2], refs[-1]
        out_refs = refs[-1 - len(outs) : -1]
        at = 0
        for i in range(count):
            rows = slice(at, at + refs[2 * i].shape[0])
            at = rows.stop
            first = pl.multiple_of(part_ref[0] * w, w)
            h_ref[rows, pl.ds(first, w)] = refs[2 * i][...]
            h_ref[rows, pl.ds(pl.multiple_of(w - first, w), w)] = refs[2 * i + 1][...]

        for i, d_ref in enumerate(weight_refs):

            @pl.loop(0, n // tile)
            def _(j):
                here = pl.multiple_of(j * tile, tile)
                out = jnp.dot(
                    h_ref[...], d_ref[:, pl.ds(here, tile)], preferred_element_type=F32
                )
                cols = pl.ds(i * n + here, tile)
                for (at, size, dtype), ref in zip(outs, out_refs):
                    ref[:, cols] = out[at : at + size].astype(dtype)

    return pl.pallas_call(
        body,
        name="down",
        in_specs=[SMEM] + [VMEM] * (2 * count + 2) + [ANY] * len(after),
        out_specs=[VMEM] * len(outs),
        out_shape=[
            jax.ShapeDtypeStruct((size, 2 * n), dtype) for _, size, dtype in outs
        ],
        scratch_shapes=[pltpu.VMEM((m, 2 * w), BF16)],
        **params(6 << 20),
    )(part, *[h for pair in halves for h in pair], *map(in_vmem, weights), *after)


def make_shards(n):
    ring = ring_of(n)
    half = n // 2
    to_right = [(ring[i], ring[(i + 1) % n]) for i in range(n)]
    to_left = [(ring[(i + 1) % n], ring[i]) for i in range(n)]
    swap = [(0, 1), (1, 0)]

    def right(x, name="right"):
        with jax.named_scope(name):
            return lax.ppermute(x, "gy", to_right)

    def left(x, name="left"):
        with jax.named_scope(name):
            return lax.ppermute(x, "gy", to_left)

    def other(x, name="swap"):
        with jax.named_scope(name):
            return lax.ppermute(x, "gx", swap)

    def add(part, block):
        return (part + block.astype(F32)).astype(BF16)

    def shards(tokens, gate_weight, up_weight, down_weight):
        rows = tokens.shape[0]
        cut = rows // 2
        core = lax.axis_index("gx").astype(jnp.int32)
        keep, give = core.reshape(1), (1 - core).reshape(1)

        a, b = tokens[:cut], tokens[cut:]
        far_r, far_l = right(a, "far_r1"), left(b, "far_l1")
        near_r, near_l = right(b, "near_r1"), left(a, "near_l1")
        wide = bring([gate_weight, up_weight], give, [])
        blocks, groups, sums, got = [[tokens]], [], [], []
        after = wide[-1:]
        for d in range(1, half):
            far_r, far_l = gate(far_r, far_l, after=after, work=GATE)
            held_r, held_l = far_r, far_l
            far_r = right(far_r, f"far_r{d + 1}")
            far_l = left(far_l, f"far_l{d + 1}")
            if d == 1:
                wide += bring([gate_weight, up_weight], keep, [held_r])
                near_r, near_l = gate(near_r, near_l, after=wide[-1:], work=GATE)
            else:
                groups.append(blocks[0] + blocks[1] if d == 2 else blocks[d - 1])
                theirs, ours = gate_up(groups[-1], wide, [held_r])
                near_r, near_l, theirs, ours, *got = gate(
                    near_r, near_l, theirs, ours, *got, work=GATE
                )
                sums.append(ours)
                if d < half - 1:
                    got.append(other(theirs, f"swap{d}"))
            blocks.append([held_r, near_r, near_l, held_l])
            if d < half - 1:
                after = [near_r]
                near_r = right(near_r, f"near_r{d + 1}")
                near_l = left(near_l, f"near_l{d + 1}")
        far_r, far_l, theirs, *got = gate(far_r, far_l, theirs, *got, after=[near_r])
        got.append(other(theirs, "swap_last"))
        last = [far_r, far_l, *blocks[-1]]

        def hide(ours, got):
            h = gated(ours, got)
            return h, other(h)

        (theirs,) = gate_up(last, wide[:2], [])
        last_got = other(theirs)
        ours, *weight = gate_up(last, wide[2:], [theirs], down_weight)
        last = hide(ours, last_got)
        near = [hide(*pair) for pair in zip(sums, got)]
        at = [(i * cut, cut) for i in range(6)]
        outs = [(*at[3], BF16), (*at[4], BF16), (*at[0], BF16), (*at[1], BF16)]
        outs += [(*at[2], F32), (*at[5], F32)]
        b_l, b_r, a_l, a_r, next_l, next_r = down([last], weight, keep, outs, [])

        b_l, b_r = left(b_l), right(b_r)
        a_l, a_r = left(a_l), right(a_r)
        (rest,) = down(near[-1:], weight, keep, [(0, 2 * rows, F32)], [next_l])
        parts = {half - 2: [rest[i * cut : (i + 1) * cut] for i in range(4)]}
        after = [rest]
        for d in range(half - 2, -1, -1):
            b_l, b_r = gate(b_l, b_r, after=after)
            if d > 0:
                _, left_b, right_a, _ = parts[d]
                b_l, b_r = add(left_b, b_l), add(right_a, b_r)
                after = [b_l, b_r]
                b_l, b_r = left(b_l), right(b_r)
            else:
                after = [b_l, b_r]
            if d == half - 2:
                size = rows * (2 * half - 5)
                (rest,) = down(near[:-1], weight, keep, [(0, size, F32)], after)
                for e in range(1, half - 2):
                    first = rows * (2 * e - 1)
                    parts[e] = [
                        rest[first + i * cut : first + (i + 1) * cut] for i in range(4)
                    ]
                after = [rest]
            a_l, a_r = gate(a_l, a_r, after=after)
            a_l, a_r = add(next_l, a_l), add(next_r, a_r)
            after = [a_l, a_r]
            a_l, a_r = left(a_l), right(a_r)
            if d > 0:
                next_l, _, _, next_r = parts[d]
        a_l, a_r = gate(a_l, a_r)
        total_a = rest[:cut] + a_l.astype(F32) + b_r.astype(F32)
        total_b = rest[cut:rows] + a_r.astype(F32) + b_l.astype(F32)
        return jnp.concatenate([total_a, total_b], axis=0).astype(BF16)

    return shards


def solution(mesh):
    return jax.shard_map(
        make_shards(mesh.shape["gy"]),
        mesh=mesh,
        in_specs=(P(("groups", "gy"), "gx"), P("gx", "gy"), P("gx", "gy"), P("gy", "gx")),
        out_specs=P(("groups", "gy"), "gx"),
        check_vma=False,
    )
```

```python
import jax
import jax.numpy as jnp
from jax import lax
from jax.experimental import pallas as pl
from jax.experimental.pallas import tpu as pltpu
from jax.sharding import PartitionSpec as P

F32, BF16 = jnp.float32, jnp.bfloat16
ANY = pl.BlockSpec(memory_space=pl.ANY)
SMEM = pl.BlockSpec(memory_space=pltpu.SMEM)
VMEM = pl.BlockSpec(memory_space=pltpu.VMEM)


def ring_of(n):
    return list(range(0, n, 2)) + list(range(n - 1, 0, -2))


def in_hbm(x):
    return pltpu.with_memory_space_constraint(x, pltpu.HBM)


def in_vmem(x):
    return pltpu.with_memory_space_constraint(x, pltpu.VMEM)


GATE, KERNEL = 22_000_000_000, 1_100_000_000


def params(vmem, work=0):
    return dict(
        compiler_params=pltpu.CompilerParams(vmem_limit_bytes=vmem),
        cost_estimate=pl.CostEstimate(flops=work, bytes_accessed=0, transcendentals=0),
    )


def gate(*arrays, after=(), work=0):
    return pl.pallas_call(
        lambda *refs: None,
        name="gate",
        in_specs=[ANY] * (len(arrays) + len(after)),
        out_specs=[ANY] * len(arrays),
        out_shape=[jax.ShapeDtypeStruct(x.shape, x.dtype) for x in arrays],
        input_output_aliases={i: i for i in range(len(arrays))},
        **params(1 << 18, work),
    )(*arrays, *after)


def fetches(sources, targets, sems, pieces=8):
    copies = []
    for i, ((source, start), target) in enumerate(zip(sources, targets)):
        step = target.shape[0] // pieces
        for s in range(pieces):
            rows = pl.ds(s * step, step)
            cols = pl.ds(start, target.shape[1])
            copies.append(
                pltpu.make_async_copy(
                    source.at[rows, cols], target.at[rows], sems.at[i, s]
                )
            )
    return copies


def bring(weights, part, after):
    k, w = weights[0].shape[0], weights[0].shape[1] // 2
    count = len(weights)

    def body(part_ref, *refs):
        start = pl.multiple_of(part_ref[0] * w, w)
        sources = [(ref, start) for ref in refs[:count]]
        copies = fetches(sources, refs[-1 - count : -1], refs[-1])
        for copy in copies:
            copy.start()
        for copy in copies:
            copy.wait()

    return pl.pallas_call(
        body,
        name="bring",
        in_specs=[SMEM] + [ANY] * (count + len(after)),
        out_specs=[VMEM] * count,
        out_shape=[pltpu.VMEM((k, w), weights[0].dtype)] * count,
        scratch_shapes=[pltpu.SemaphoreType.DMA((count, 8))],
        **params(1 << 18, KERNEL),
    )(part, *map(in_hbm, weights), *after)


def gate_up(pieces, weights, after, load=None, side=0):
    if any(p.shape[0] % 16 for p in pieces):
        pieces = [jnp.concatenate(pieces, axis=0)]
    m, k = sum(p.shape[0] for p in pieces), pieces[0].shape[1]
    w = weights[0].shape[1]
    tile = min(w, 256)
    count, halves = len(pieces), len(weights) // 2
    shapes = [jax.ShapeDtypeStruct((2, m, w), F32)] * halves
    scratch = [pltpu.VMEM((m, k), BF16)]
    extra = []
    if load is not None:
        wide = load.shape[1] // 2
        extra = [in_hbm(load)]
        shapes += [pltpu.VMEM((load.shape[0], wide), load.dtype)]
        scratch += [pltpu.SemaphoreType.DMA((1, 8))]

    def body(*refs):
        weight_refs = refs[count : count + len(weights)]
        outs = refs[-len(shapes) - len(scratch) : -len(scratch)]
        out_refs, x_ref = outs[:halves], refs[-len(scratch)]
        copies = []
        if load is not None:
            source = refs[count + len(weights)]
            copies = fetches([(source, side * wide)], outs[halves:], refs[-1])
        for copy in copies:
            copy.start()
        at = 0
        for ref in refs[:count]:
            x_ref[at : at + ref.shape[0]] = ref[...]
            at += ref.shape[0]

        @pl.loop(0, w // tile)
        def _(j):
            cols = pl.ds(pl.multiple_of(j * tile, tile), tile)
            for i, ref in enumerate(weight_refs):
                out_refs[i // 2][i % 2, :, cols] = jnp.dot(
                    x_ref[...], ref[:, cols], preferred_element_type=F32
                )

        for copy in copies:
            copy.wait()

    return pl.pallas_call(
        body,
        name="gate_up",
        in_specs=[VMEM] * (count + len(weights)) + [ANY] * (len(extra) + len(after)),
        out_specs=[VMEM] * len(shapes),
        out_shape=shapes,
        scratch_shapes=scratch,
        **params(3 << 20, KERNEL),
    )(*pieces, *map(in_vmem, weights), *extra, *after)


def gated(ours, theirs):
    _, m, w = ours.shape
    tile = min(w, 256)

    def body(a_ref, b_ref, o_ref):
        @pl.loop(0, w // tile)
        def _(j):
            cols = pl.ds(pl.multiple_of(j * tile, tile), tile)
            v = a_ref[0, :, cols] + b_ref[0, :, cols]
            u = a_ref[1, :, cols] + b_ref[1, :, cols]
            o_ref[:, cols] = (v / (1.0 + jnp.exp(-v)) * u).astype(BF16)

    return pl.pallas_call(
        body,
        name="gated",
        in_specs=[VMEM, VMEM],
        out_specs=VMEM,
        out_shape=jax.ShapeDtypeStruct((m, w), BF16),
        **params(2 << 20),
    )(ours, theirs)


def down(halves, weights, part, outs, after):
    m = sum(h.shape[0] for h, _ in halves)
    w = halves[0][0].shape[1]
    n = weights[0].shape[1]
    tile = 512
    if any(h.shape[0] % 16 for h, _ in halves):
        halves = [tuple(jnp.concatenate(hs, axis=0) for hs in zip(*halves))]
    count = len(halves)

    def body(part_ref, *refs):
        weight_refs, h_ref = refs[2 * count : 2 * count + 2], refs[-1]
        out_refs = refs[-1 - len(outs) : -1]
        at = 0
        for i in range(count):
            rows = slice(at, at + refs[2 * i].shape[0])
            at = rows.stop
            first = pl.multiple_of(part_ref[0] * w, w)
            h_ref[rows, pl.ds(first, w)] = refs[2 * i][...]
            h_ref[rows, pl.ds(pl.multiple_of(w - first, w), w)] = refs[2 * i + 1][...]

        for i, d_ref in enumerate(weight_refs):

            @pl.loop(0, n // tile)
            def _(j):
                here = pl.multiple_of(j * tile, tile)
                out = jnp.dot(
                    h_ref[...], d_ref[:, pl.ds(here, tile)], preferred_element_type=F32
                )
                cols = pl.ds(i * n + here, tile)
                for (at, size, dtype), ref in zip(outs, out_refs):
                    ref[:, cols] = out[at : at + size].astype(dtype)

    return pl.pallas_call(
        body,
        name="down",
        in_specs=[SMEM] + [VMEM] * (2 * count + 2) + [ANY] * len(after),
        out_specs=[VMEM] * len(outs),
        out_shape=[
            jax.ShapeDtypeStruct((size, 2 * n), dtype) for _, size, dtype in outs
        ],
        scratch_shapes=[pltpu.VMEM((m, 2 * w), BF16)],
        **params(3 << 20),
    )(part, *[h for pair in halves for h in pair], *map(in_vmem, weights), *after)


def make_shards(n):
    ring = ring_of(n)
    half = n // 2
    to_right = [(ring[i], ring[(i + 1) % n]) for i in range(n)]
    to_left = [(ring[(i + 1) % n], ring[i]) for i in range(n)]
    swap = [(0, 1), (1, 0)]

    def right(x, name="right"):
        with jax.named_scope(name):
            return lax.ppermute(x, "gy", to_right)

    def left(x, name="left"):
        with jax.named_scope(name):
            return lax.ppermute(x, "gy", to_left)

    def other(x, name="swap"):
        with jax.named_scope(name):
            return lax.ppermute(x, "gx", swap)

    def add(part, block):
        return (part + block.astype(F32)).astype(BF16)

    def shards(tokens, gate_weight, up_weight, down_weight):
        rows = tokens.shape[0]
        cut = rows // 2
        core = lax.axis_index("gx").astype(jnp.int32)
        keep, give = core.reshape(1), (1 - core).reshape(1)

        a, b = tokens[:cut], tokens[cut:]
        far_r, far_l = right(a, "farR1"), left(b, "farL1")
        wide = bring([gate_weight], give, [])
        near_r, near_l = right(b, "nearR1"), left(a, "nearL1")
        wide += bring([up_weight], give, wide)
        waiting = {("own", 0): tokens}
        groups, theirs, ours = [], [], []
        after = wide[-1:]
        for d in range(1, half):
            far_r, far_l = gate(far_r, far_l, after=after, work=GATE)
            held = {("far_r", d): far_r, ("far_l", d): far_l}
            after = [far_r]
            far_r, far_l = right(far_r, f"farR{d + 1}"), left(far_l, f"farL{d + 1}")
            if d == 1:
                wide += bring([gate_weight, up_weight], keep, after)
                done = wide[-1:]
            else:
                if d > 2:
                    waiting |= held
                out = gate_up(list(waiting.values()), wide, after)
                groups.append(list(waiting))
                theirs.append(out[0])
                ours.append(out[1])
                done, waiting = out[:1], {}
            if d <= 2:
                waiting |= held
            near_r, near_l = gate(near_r, near_l, after=done, work=GATE)
            waiting |= {("near_r", d): near_r, ("near_l", d): near_l}
            after = [near_r]
            if d < half - 1:
                near_r = right(near_r, f"nearR{d + 1}")
                near_l = left(near_l, f"nearL{d + 1}")
        far_r, far_l, *theirs = gate(far_r, far_l, *theirs, after=after)
        got = [other(x) for x in theirs]
        waiting |= {("far_r", half): far_r, ("far_l", half): far_l}

        def hide(ours, got):
            h = gated(ours, got)
            return h, other(h)

        last = list(waiting.values())
        last_theirs, low = gate_up(last, wide[:2], [], down_weight, 0)
        last_got = other(last_theirs)
        last_ours, high = gate_up(last, wide[2:], [last_theirs], down_weight, 1)
        weight = [low, high]
        last = hide(last_ours, last_got)
        outs = [(i * cut, cut, BF16) for i in range(4)]
        b_l, b_r, a_l, a_r = down([last], weight, keep, outs, [])
        hidden = [hide(*pair) for pair in zip(ours, got)]

        def put_down(which, after):
            size = sum(h.shape[0] for h, _ in hidden[which])
            outs = [(0, size, F32)]
            (rest,) = down(hidden[which], weight, keep, outs, after)
            at = 0
            for key in sum(groups[which], []):
                part[key] = rest[at : at + (rows if key[0] == "own" else cut)]
                at += part[key].shape[0]
            return rest

        part = {}
        b_l, b_r = left(b_l), right(b_r)
        a_l, a_r = left(a_l), right(a_r)
        after = [put_down(slice(-1, None), [])]
        for d in range(half - 1, 0, -1):
            b_l, b_r = gate(b_l, b_r, after=after)
            if d > 1:
                b_l = add(part["near_r", d - 1], b_l)
                b_r = add(part["near_l", d - 1], b_r)
                after = [b_l, b_r]
                b_l, b_r = left(b_l), right(b_r)
            else:
                after = [b_l, b_r]
            if d == half - 1:
                after = [put_down(slice(0, -1), after)]
            a_l, a_r = gate(a_l, a_r, after=after)
            a_l, a_r = add(part["far_r", d], a_l), add(part["far_l", d], a_r)
            after = [a_l, a_r]
            a_l, a_r = left(a_l), right(a_r)
        a_l, a_r = gate(a_l, a_r)
        own = part["own", 0]
        total_a = own[:cut] + a_l.astype(F32) + b_r.astype(F32)
        total_b = own[cut:] + a_r.astype(F32) + b_l.astype(F32)
        return jnp.concatenate([total_a, total_b], axis=0).astype(BF16)

    return shards


def solution(mesh):
    return jax.shard_map(
        make_shards(mesh.shape["gy"]),
        mesh=mesh,
        in_specs=(P(("groups", "gy"), "gx"), P("gx", "gy"), P("gx", "gy"), P("gy", "gx")),
        out_specs=P(("groups", "gy"), "gx"),
        check_vma=False,
    )
```

```python
import jax
import jax.numpy as jnp
from jax import lax
from jax.experimental import pallas as pl
from jax.experimental.pallas import tpu as pltpu
from jax.sharding import PartitionSpec as P

F32, BF16 = jnp.float32, jnp.bfloat16
ANY = pl.BlockSpec(memory_space=pl.ANY)
SMEM = pl.BlockSpec(memory_space=pltpu.SMEM)
VMEM = pl.BlockSpec(memory_space=pltpu.VMEM)


def ring_of(n):
    return list(range(0, n, 2)) + list(range(n - 1, 0, -2))


def in_hbm(x):
    return pltpu.with_memory_space_constraint(x, pltpu.HBM)


def in_vmem(x):
    return pltpu.with_memory_space_constraint(x, pltpu.VMEM)


GATE, KERNEL = 22_000_000_000, 1_100_000_000


def params(vmem, work=0):
    return dict(
        compiler_params=pltpu.CompilerParams(vmem_limit_bytes=vmem),
        cost_estimate=pl.CostEstimate(flops=work, bytes_accessed=0, transcendentals=0),
    )


def gate(*arrays, after=(), work=0):
    return pl.pallas_call(
        lambda *refs: None,
        name="gate",
        in_specs=[ANY] * (len(arrays) + len(after)),
        out_specs=[ANY] * len(arrays),
        out_shape=[jax.ShapeDtypeStruct(x.shape, x.dtype) for x in arrays],
        input_output_aliases={i: i for i in range(len(arrays))},
        **params(1 << 18, work),
    )(*arrays, *after)


def fetches(sources, targets, sems, pieces=8):
    copies = []
    for i, ((source, start), target) in enumerate(zip(sources, targets)):
        step = target.shape[0] // pieces
        for s in range(pieces):
            rows = pl.ds(s * step, step)
            cols = pl.ds(start, target.shape[1])
            copies.append(
                pltpu.make_async_copy(
                    source.at[rows, cols], target.at[rows], sems.at[i, s]
                )
            )
    return copies


def bring(weights, part, after):
    k, w = weights[0].shape[0], weights[0].shape[1] // 2
    count = len(weights)

    def body(part_ref, *refs):
        start = pl.multiple_of(part_ref[0] * w, w)
        sources = [(ref, start) for ref in refs[:count]]
        copies = fetches(sources, refs[-1 - count : -1], refs[-1])
        for copy in copies:
            copy.start()
        for copy in copies:
            copy.wait()

    return pl.pallas_call(
        body,
        name="bring",
        in_specs=[SMEM] + [ANY] * (count + len(after)),
        out_specs=[VMEM] * count,
        out_shape=[pltpu.VMEM((k, w), weights[0].dtype)] * count,
        scratch_shapes=[pltpu.SemaphoreType.DMA((count, 8))],
        **params(1 << 18, KERNEL),
    )(part, *map(in_hbm, weights), *after)


def gate_up(pieces, weights, after, load=None, side=0):
    if any(p.shape[0] % 16 for p in pieces):
        pieces = [jnp.concatenate(pieces, axis=0)]
    m, k = sum(p.shape[0] for p in pieces), pieces[0].shape[1]
    w = weights[0].shape[1]
    tile = min(w, 256)
    count, halves = len(pieces), len(weights) // 2
    shapes = [jax.ShapeDtypeStruct((2, m, w), F32)] * halves
    scratch = [pltpu.VMEM((m, k), BF16)]
    extra = []
    if load is not None:
        wide = load.shape[1] // 2
        extra = [in_hbm(load)]
        shapes += [pltpu.VMEM((load.shape[0], wide), load.dtype)]
        scratch += [pltpu.SemaphoreType.DMA((1, 8))]

    def body(*refs):
        weight_refs = refs[count : count + len(weights)]
        outs = refs[-len(shapes) - len(scratch) : -len(scratch)]
        out_refs, x_ref = outs[:halves], refs[-len(scratch)]
        copies = []
        if load is not None:
            source = refs[count + len(weights)]
            copies = fetches([(source, side * wide)], outs[halves:], refs[-1])
        for copy in copies:
            copy.start()
        at = 0
        for ref in refs[:count]:
            x_ref[at : at + ref.shape[0]] = ref[...]
            at += ref.shape[0]

        @pl.loop(0, w // tile)
        def _(j):
            cols = pl.ds(pl.multiple_of(j * tile, tile), tile)
            for i, ref in enumerate(weight_refs):
                out_refs[i // 2][i % 2, :, cols] = jnp.dot(
                    x_ref[...], ref[:, cols], preferred_element_type=F32
                )

        for copy in copies:
            copy.wait()

    return pl.pallas_call(
        body,
        name="gate_up",
        in_specs=[VMEM] * (count + len(weights)) + [ANY] * (len(extra) + len(after)),
        out_specs=[VMEM] * len(shapes),
        out_shape=shapes,
        scratch_shapes=scratch,
        **params(3 << 20, KERNEL),
    )(*pieces, *map(in_vmem, weights), *extra, *after)


def gated(ours, theirs):
    _, m, w = ours.shape
    tile = min(w, 256)

    def body(a_ref, b_ref, o_ref):
        @pl.loop(0, w // tile)
        def _(j):
            cols = pl.ds(pl.multiple_of(j * tile, tile), tile)
            v = a_ref[0, :, cols] + b_ref[0, :, cols]
            u = a_ref[1, :, cols] + b_ref[1, :, cols]
            o_ref[:, cols] = (v / (1.0 + jnp.exp(-v)) * u).astype(BF16)

    return pl.pallas_call(
        body,
        name="gated",
        in_specs=[VMEM, VMEM],
        out_specs=VMEM,
        out_shape=jax.ShapeDtypeStruct((m, w), BF16),
        **params(2 << 20),
    )(ours, theirs)


def down(halves, weights, part, outs, after):
    m = sum(h.shape[0] for h, _ in halves)
    w = halves[0][0].shape[1]
    n = weights[0].shape[1]
    tile = 512
    if any(h.shape[0] % 16 for h, _ in halves):
        halves = [tuple(jnp.concatenate(hs, axis=0) for hs in zip(*halves))]
    count = len(halves)

    def body(part_ref, *refs):
        weight_refs, h_ref = refs[2 * count : 2 * count + 2], refs[-1]
        out_refs = refs[-1 - len(outs) : -1]
        at = 0
        for i in range(count):
            rows = slice(at, at + refs[2 * i].shape[0])
            at = rows.stop
            first = pl.multiple_of(part_ref[0] * w, w)
            h_ref[rows, pl.ds(first, w)] = refs[2 * i][...]
            h_ref[rows, pl.ds(pl.multiple_of(w - first, w), w)] = refs[2 * i + 1][...]

        for i, d_ref in enumerate(weight_refs):

            @pl.loop(0, n // tile)
            def _(j):
                here = pl.multiple_of(j * tile, tile)
                out = jnp.dot(
                    h_ref[...], d_ref[:, pl.ds(here, tile)], preferred_element_type=F32
                )
                cols = pl.ds(i * n + here, tile)
                for (at, size, dtype), ref in zip(outs, out_refs):
                    ref[:, cols] = out[at : at + size].astype(dtype)

    return pl.pallas_call(
        body,
        name="down",
        in_specs=[SMEM] + [VMEM] * (2 * count + 2) + [ANY] * len(after),
        out_specs=[VMEM] * len(outs),
        out_shape=[
            jax.ShapeDtypeStruct((size, 2 * n), dtype) for _, size, dtype in outs
        ],
        scratch_shapes=[pltpu.VMEM((m, 2 * w), BF16)],
        **params(3 << 20),
    )(part, *[h for pair in halves for h in pair], *map(in_vmem, weights), *after)


def make_shards(n):
    ring = ring_of(n)
    half = n // 2
    to_right = [(ring[i], ring[(i + 1) % n]) for i in range(n)]
    to_left = [(ring[(i + 1) % n], ring[i]) for i in range(n)]
    swap = [(0, 1), (1, 0)]

    def right(x, name="right"):
        with jax.named_scope(name):
            return lax.ppermute(x, "gy", to_right)

    def left(x, name="left"):
        with jax.named_scope(name):
            return lax.ppermute(x, "gy", to_left)

    def other(x, name="swap"):
        with jax.named_scope(name):
            return lax.ppermute(x, "gx", swap)

    def add(part, block):
        return (part + block.astype(F32)).astype(BF16)

    def shards(tokens, gate_weight, up_weight, down_weight):
        rows = tokens.shape[0]
        cut = rows // 2
        core = lax.axis_index("gx").astype(jnp.int32)
        keep, give = core.reshape(1), (1 - core).reshape(1)

        a, b = tokens[:cut], tokens[cut:]
        far_r, far_l = right(a, "farR1"), left(b, "farL1")
        wide = bring([gate_weight], give, [])
        near_r, near_l = right(b, "nearR1"), left(a, "nearL1")
        wide += bring([up_weight], give, wide)
        waiting = {("own", "a"): a, ("own", "b"): b}
        groups, theirs, ours = [], [], []
        after = wide[-1:]
        for d in range(1, half):
            far_r, far_l = gate(far_r, far_l, after=after, work=GATE)
            held = {("far_r", d): far_r, ("far_l", d): far_l}
            after = [far_r]
            far_r, far_l = right(far_r, f"farR{d + 1}"), left(far_l, f"farL{d + 1}")
            if d > 2:
                waiting |= held
            if d == 1:
                wide += bring([gate_weight, up_weight], keep, after)
                done = wide[-1:]
            else:
                groups.append(list(waiting))
                rows_now, waiting = list(waiting.values()), {}
                both = True
                out = gate_up(rows_now, wide if both else wide[:2], after)
                theirs.append(out[0])
                ours += out[1:]
                done = out[:1]
            if d <= 2:
                waiting |= held
            near_r, near_l = gate(near_r, near_l, after=done, work=GATE)
            waiting |= {("near_r", d): near_r, ("near_l", d): near_l}
            after = [near_r]
            if d < half - 1:
                near_r = right(near_r, f"nearR{d + 1}")
                near_l = left(near_l, f"nearL{d + 1}")
                if d > 1 and not both:
                    ours += gate_up(rows_now, wide[2:], after)
                    after = ours[-1:]
        far_r, far_l, *theirs = gate(far_r, far_l, *theirs, after=after)
        waiting |= {("far_r", half): far_r, ("far_l", half): far_l}

        def hide(ours, got):
            h = gated(ours, got)
            return h, other(h)

        last = list(waiting.values())
        last_theirs, low = gate_up(last, wide[:2], [], down_weight, 0)
        last_got = other(last_theirs)
        got = [other(x) for x in theirs]
        last_ours, high = gate_up(last, wide[2:], [last_theirs], down_weight, 1)
        weight = [low, high]
        last = hide(last_ours, last_got)
        outs = [(i * cut, cut, BF16) for i in range(4)]
        b_l, b_r, a_l, a_r = down([last], weight, keep, outs, [])
        hidden = [hide(*pair) for pair in zip(ours, got)]

        def put_down(which, after):
            size = sum(h.shape[0] for h, _ in hidden[which])
            outs = [(0, size, F32)]
            (rest,) = down(hidden[which], weight, keep, outs, after)
            at = 0
            for key in sum(groups[which], []):
                part[key] = rest[at : at + cut]
                at += cut
            return rest

        part = {}
        a_l, a_r = left(a_l), right(a_r)
        b_l, b_r = left(b_l), right(b_r)
        after = [put_down(slice(-1, None), [])]
        for d in range(half - 1, 0, -1):
            a_l, a_r = gate(a_l, a_r, after=after)
            a_l, a_r = add(part["far_r", d], a_l), add(part["far_l", d], a_r)
            after = [a_l, a_r]
            a_l, a_r = left(a_l), right(a_r)
            b_l, b_r = gate(b_l, b_r, after=after)
            if d > 1:
                b_l = add(part["near_r", d - 1], b_l)
                b_r = add(part["near_l", d - 1], b_r)
                after = [b_l, b_r]
                b_l, b_r = left(b_l), right(b_r)
            if d == half - 1:
                after = [put_down(slice(0, -1), after)]
        a_l, a_r = gate(a_l, a_r, after=[b_l])
        total_a = part["own", "a"] + a_l.astype(F32) + b_r.astype(F32)
        total_b = part["own", "b"] + a_r.astype(F32) + b_l.astype(F32)
        return jnp.concatenate([total_a, total_b], axis=0).astype(BF16)

    return shards


def solution(mesh):
    return jax.shard_map(
        make_shards(mesh.shape["gy"]),
        mesh=mesh,
        in_specs=(P(("groups", "gy"), "gx"), P("gx", "gy"), P("gx", "gy"), P("gy", "gx")),
        out_specs=P(("groups", "gy"), "gx"),
        check_vma=False,
    )
```

```python
import jax
import jax.numpy as jnp
from jax import lax
from jax.experimental import pallas as pl
from jax.experimental.pallas import tpu as pltpu
from jax.sharding import PartitionSpec as P

F32, BF16 = jnp.float32, jnp.bfloat16
ANY = pl.BlockSpec(memory_space=pl.ANY)
VMEM = pl.BlockSpec(memory_space=pltpu.VMEM)


def ring_of(n):
    return list(range(0, n, 2)) + list(range(n - 1, 0, -2))


def in_hbm(x):
    return pltpu.with_memory_space_constraint(x, pltpu.HBM)


def in_vmem(x):
    return pltpu.with_memory_space_constraint(x, pltpu.VMEM)


GATE, KERNEL = 22_000_000_000, 1_100_000_000


def params(vmem, work=0):
    return dict(
        compiler_params=pltpu.CompilerParams(vmem_limit_bytes=vmem),
        cost_estimate=pl.CostEstimate(flops=work, bytes_accessed=0, transcendentals=0),
    )


def gate(*arrays, after=(), work=0):
    return pl.pallas_call(
        lambda *refs: None,
        name="gate",
        in_specs=[ANY] * (len(arrays) + len(after)),
        out_specs=[ANY] * len(arrays),
        out_shape=[jax.ShapeDtypeStruct(x.shape, x.dtype) for x in arrays],
        input_output_aliases={i: i for i in range(len(arrays))},
        **params(1 << 18, work),
    )(*arrays, *after)


def fetches(sources, targets, sems, pieces=8):
    copies = []
    for i, ((source, start), target) in enumerate(zip(sources, targets)):
        step = target.shape[0] // pieces
        for s in range(pieces):
            rows = pl.ds(s * step, step)
            cols = pl.ds(start, target.shape[1])
            copies.append(
                pltpu.make_async_copy(
                    source.at[rows, cols], target.at[rows], sems.at[i, s]
                )
            )
    return copies


def half_of(mine, w):
    core = lax.axis_index("gx")
    return pl.multiple_of((core if mine else 1 - core) * w, w)


def bring(weights, mine, after):
    k, w = weights[0].shape[0], weights[0].shape[1] // 2
    count = len(weights)

    def body(*refs):
        sources = [(ref, half_of(mine, w)) for ref in refs[:count]]
        copies = fetches(sources, refs[-1 - count : -1], refs[-1])
        for copy in copies:
            copy.start()
        for copy in copies:
            copy.wait()

    return pl.pallas_call(
        body,
        name="bring",
        in_specs=[ANY] * (count + len(after)),
        out_specs=[VMEM] * count,
        out_shape=[pltpu.VMEM((k, w), weights[0].dtype)] * count,
        scratch_shapes=[pltpu.SemaphoreType.DMA((count, 8))],
        **params(1 << 18, KERNEL),
    )(*map(in_hbm, weights), *after)


def gate_up(pieces, weights, after, load=()):
    if any(p.shape[0] % 16 for p in pieces):
        pieces = [jnp.concatenate(pieces, axis=0)]
    m, k = sum(p.shape[0] for p in pieces), pieces[0].shape[1]
    w = weights[0].shape[1]
    tile = min(w, 512)
    count, halves = len(pieces), len(weights) // 2
    shapes = [jax.ShapeDtypeStruct((2, m, w), F32)] * halves
    scratch = [pltpu.VMEM((m, k), BF16)]
    for x, _ in load:
        shapes.append(pltpu.VMEM((x.shape[0], x.shape[1] // 2), x.dtype))
    if load:
        scratch.append(pltpu.SemaphoreType.DMA((len(load), 8)))

    def body(*refs):
        weight_refs = refs[count : count + len(weights)]
        outs = refs[-len(shapes) - len(scratch) : -len(scratch)]
        out_refs, x_ref = outs[:halves], refs[-len(scratch)]
        copies = []
        if load:
            sources = refs[count + len(weights) :]
            starts = [
                half_of(True, w) if which == "own" else which * (x.shape[1] // 2)
                for x, which in load
            ]
            copies = fetches(list(zip(sources, starts)), outs[halves:], refs[-1])
        for copy in copies:
            copy.start()
        at = 0
        for ref in refs[:count]:
            x_ref[at : at + ref.shape[0]] = ref[...]
            at += ref.shape[0]

        @pl.loop(0, w // tile)
        def _(j):
            cols = pl.ds(pl.multiple_of(j * tile, tile), tile)
            for i, ref in enumerate(weight_refs):
                out_refs[i // 2][i % 2, :, cols] = jnp.dot(
                    x_ref[...], ref[:, cols], preferred_element_type=F32
                )

        for copy in copies:
            copy.wait()

    return pl.pallas_call(
        body,
        name="gate_up",
        in_specs=[VMEM] * (count + len(weights)) + [ANY] * (len(load) + len(after)),
        out_specs=[VMEM] * len(shapes),
        out_shape=shapes,
        scratch_shapes=scratch,
        **params(3 << 20, KERNEL),
    )(*pieces, *map(in_vmem, weights), *[in_hbm(x) for x, _ in load], *after)


def gated(ours, theirs):
    _, m, w = ours.shape
    tile = min(w, 256)

    def body(a_ref, b_ref, o_ref):
        @pl.loop(0, w // tile)
        def _(j):
            cols = pl.ds(pl.multiple_of(j * tile, tile), tile)
            v = a_ref[0, :, cols] + b_ref[0, :, cols]
            u = a_ref[1, :, cols] + b_ref[1, :, cols]
            o_ref[:, cols] = (v / (1.0 + jnp.exp(-v)) * u).astype(BF16)

    return pl.pallas_call(
        body,
        name="gated",
        in_specs=[VMEM, VMEM],
        out_specs=VMEM,
        out_shape=jax.ShapeDtypeStruct((m, w), BF16),
        **params(2 << 20),
    )(ours, theirs)


def down(halves, weights, outs, after):
    m = sum(h.shape[0] for h, _ in halves)
    w = halves[0][0].shape[1]
    n = weights[0].shape[1]
    tile = 512
    if any(h.shape[0] % 16 for h, _ in halves):
        halves = [tuple(jnp.concatenate(hs, axis=0) for hs in zip(*halves))]
    count = len(halves)

    def body(*refs):
        weight_refs, h_ref = refs[2 * count : 2 * count + 2], refs[-1]
        out_refs = refs[-1 - len(outs) : -1]
        at = 0
        for i in range(count):
            rows = slice(at, at + refs[2 * i].shape[0])
            at = rows.stop
            h_ref[rows, pl.ds(half_of(True, w), w)] = refs[2 * i][...]
            h_ref[rows, pl.ds(half_of(False, w), w)] = refs[2 * i + 1][...]

        for i, d_ref in enumerate(weight_refs):

            @pl.loop(0, n // tile)
            def _(j):
                here = pl.multiple_of(j * tile, tile)
                out = jnp.dot(
                    h_ref[...], d_ref[:, pl.ds(here, tile)], preferred_element_type=F32
                )
                cols = pl.ds(i * n + here, tile)
                for (at, size, dtype), ref in zip(outs, out_refs):
                    ref[:, cols] = out[at : at + size].astype(dtype)

    return pl.pallas_call(
        body,
        name="down",
        in_specs=[VMEM] * (2 * count + 2) + [ANY] * len(after),
        out_specs=[VMEM] * len(outs),
        out_shape=[
            jax.ShapeDtypeStruct((size, 2 * n), dtype) for _, size, dtype in outs
        ],
        scratch_shapes=[pltpu.VMEM((m, 2 * w), BF16)],
        **params(3 << 20),
    )(*[h for pair in halves for h in pair], *map(in_vmem, weights), *after)


def make_shards(n):
    ring = ring_of(n)
    half = n // 2
    to_right = [(ring[i], ring[(i + 1) % n]) for i in range(n)]
    to_left = [(ring[(i + 1) % n], ring[i]) for i in range(n)]
    swap = [(0, 1), (1, 0)]

    def right(x, name="right"):
        with jax.named_scope(name):
            return lax.ppermute(x, "gy", to_right)

    def left(x, name="left"):
        with jax.named_scope(name):
            return lax.ppermute(x, "gy", to_left)

    def other(x, name="swap"):
        with jax.named_scope(name):
            return lax.ppermute(x, "gx", swap)

    def add(part, block):
        return (part + block.astype(F32)).astype(BF16)

    def shards(tokens, gate_weight, up_weight, down_weight):
        rows = tokens.shape[0]
        cut = rows // 2

        a, b = tokens[:cut], tokens[cut:]
        far_r, far_l = right(a, "farR1"), left(b, "farL1")
        wide = bring([gate_weight], False, [])
        near_r, near_l = right(b, "nearR1"), left(a, "nearL1")
        wide += bring([up_weight], False, wide)
        groups, theirs, ours = [], [], []
        after = wide[-1:]
        for d in range(1, half):
            far_r, far_l = gate(far_r, far_l, after=after, work=GATE)
            held = {("far_r", d): far_r, ("far_l", d): far_l}
            after = [far_r]
            far_r, far_l = right(far_r, f"farR{d + 1}"), left(far_l, f"farL{d + 1}")
            if d == 1:
                waiting = {("own", "a"): a, ("own", "b"): b} | held
                done = after
            elif d == 2:
                ours += gate_up(rows_now, wide[2:], after)
                waiting, done = held, ours[-1:]
            else:
                waiting |= held
                groups.append(list(waiting))
                out = gate_up(list(waiting.values()), wide, after)
                theirs.append(out[0])
                ours.append(out[1])
                waiting, done = {}, out[:1]
            near_r, near_l = gate(near_r, near_l, after=done, work=GATE)
            waiting |= {("near_r", d): near_r, ("near_l", d): near_l}
            after = [near_r]
            if d < half - 1:
                near_r = right(near_r, f"nearR{d + 1}")
                near_l = left(near_l, f"nearL{d + 1}")
            if d == 1:
                groups.append(list(waiting))
                rows_now = list(waiting.values())
                load = [(gate_weight, "own"), (up_weight, "own")]
                out = gate_up(rows_now, wide, after, load)
                theirs.append(out[0])
                wide += out[1:]
                after = out[:1]
        far_r, far_l, *theirs = gate(far_r, far_l, *theirs, after=after)
        waiting |= {("far_r", half): far_r, ("far_l", half): far_l}

        def hide(ours, got):
            h = gated(ours, got)
            return h, other(h)

        last = list(waiting.values())
        last_theirs, low = gate_up(last, wide[:2], [], [(down_weight, 0)])
        last_got = other(last_theirs)
        got = [other(x) for x in theirs]
        last_ours, high = gate_up(last, wide[2:], [last_theirs], [(down_weight, 1)])
        weight = [low, high]
        last = hide(last_ours, last_got)
        outs = [(i * cut, cut, BF16) for i in range(4)]
        b_l, b_r, a_l, a_r = down([last], weight, outs, [])
        hidden = [hide(*pair) for pair in zip(ours, got)]

        def put_down(which, after):
            size = sum(h.shape[0] for h, _ in hidden[which])
            outs = [(0, size, F32)]
            (rest,) = down(hidden[which], weight, outs, after)
            at = 0
            for key in sum(groups[which], []):
                part[key] = rest[at : at + cut]
                at += cut
            return rest

        part = {}
        a_l, a_r = left(a_l), right(a_r)
        b_l, b_r = left(b_l), right(b_r)
        after = [put_down(slice(-1, None), [])]
        for d in range(half - 1, 0, -1):
            a_l, a_r = gate(a_l, a_r, after=after)
            a_l, a_r = add(part["far_r", d], a_l), add(part["far_l", d], a_r)
            after = [a_l, a_r]
            a_l, a_r = left(a_l), right(a_r)
            b_l, b_r = gate(b_l, b_r, after=after)
            if d > 1:
                b_l = add(part["near_r", d - 1], b_l)
                b_r = add(part["near_l", d - 1], b_r)
                after = [b_l, b_r]
                b_l, b_r = left(b_l), right(b_r)
            if d == half - 1:
                after = [put_down(slice(0, -1), after)]
        a_l, a_r = gate(a_l, a_r, after=[b_l])
        total_a = part["own", "a"] + a_l.astype(F32) + b_r.astype(F32)
        total_b = part["own", "b"] + a_r.astype(F32) + b_l.astype(F32)
        return jnp.concatenate([total_a, total_b], axis=0).astype(BF16)

    return shards


def solution(mesh):
    return jax.shard_map(
        make_shards(mesh.shape["gy"]),
        mesh=mesh,
        in_specs=(P(("groups", "gy"), "gx"), P("gx", "gy"), P("gx", "gy"), P("gy", "gx")),
        out_specs=P(("groups", "gy"), "gx"),
        check_vma=False,
    )
```

```python
import jax
import jax.numpy as jnp
from jax import lax
from jax.experimental import pallas as pl
from jax.experimental.pallas import tpu as pltpu
from jax.sharding import PartitionSpec as P

F32, BF16 = jnp.float32, jnp.bfloat16
ANY = pl.BlockSpec(memory_space=pl.ANY)
VMEM = pl.BlockSpec(memory_space=pltpu.VMEM)


def ring_of(n):
    return list(range(0, n, 2)) + list(range(n - 1, 0, -2))


def in_hbm(x):
    return pltpu.with_memory_space_constraint(x, pltpu.HBM)


def in_vmem(x):
    return pltpu.with_memory_space_constraint(x, pltpu.VMEM)


GATE, KERNEL = 22_000_000_000, 1_100_000_000


def params(vmem, work=0):
    return dict(
        compiler_params=pltpu.CompilerParams(vmem_limit_bytes=vmem),
        cost_estimate=pl.CostEstimate(flops=work, bytes_accessed=0, transcendentals=0),
    )


def gate(*arrays, after=(), work=0):
    return pl.pallas_call(
        lambda *refs: None,
        name="gate",
        in_specs=[ANY] * (len(arrays) + len(after)),
        out_specs=[ANY] * len(arrays),
        out_shape=[jax.ShapeDtypeStruct(x.shape, x.dtype) for x in arrays],
        input_output_aliases={i: i for i in range(len(arrays))},
        **params(1 << 18, work),
    )(*arrays, *after)


def fetches(sources, targets, sems, pieces=8):
    copies = []
    for i, ((source, start), target) in enumerate(zip(sources, targets)):
        step = target.shape[0] // pieces
        for s in range(pieces):
            rows = pl.ds(s * step, step)
            cols = pl.ds(start, target.shape[1])
            copies.append(
                pltpu.make_async_copy(
                    source.at[rows, cols], target.at[rows], sems.at[i, s]
                )
            )
    return copies


def half_of(mine, w):
    core = lax.axis_index("gx")
    return pl.multiple_of((core if mine else 1 - core) * w, w)


def bring(weights, mine, after):
    k, w = weights[0].shape[0], weights[0].shape[1] // 2
    count = len(weights)

    def body(*refs):
        sources = [(ref, half_of(mine, w)) for ref in refs[:count]]
        copies = fetches(sources, refs[-1 - count : -1], refs[-1])
        for copy in copies:
            copy.start()
        for copy in copies:
            copy.wait()

    return pl.pallas_call(
        body,
        name="bring",
        in_specs=[ANY] * (count + len(after)),
        out_specs=[VMEM] * count,
        out_shape=[pltpu.VMEM((k, w), weights[0].dtype)] * count,
        scratch_shapes=[pltpu.SemaphoreType.DMA((count, 8))],
        **params(1 << 18, KERNEL),
    )(*map(in_hbm, weights), *after)


def gate_up(pieces, weights, after, load=()):
    if any(p.shape[0] % 16 for p in pieces):
        pieces = [jnp.concatenate(pieces, axis=0)]
    m, k = sum(p.shape[0] for p in pieces), pieces[0].shape[1]
    w = weights[0].shape[1]
    tile = min(w, 1024)
    count, halves = len(pieces), len(weights) // 2
    shapes = [jax.ShapeDtypeStruct((2, m, w), F32)] * halves
    scratch = [pltpu.VMEM((m, k), BF16)]
    for x, _ in load:
        shapes.append(pltpu.VMEM((x.shape[0], x.shape[1] // 2), x.dtype))
    if load:
        scratch.append(pltpu.SemaphoreType.DMA((len(load), 8)))

    def body(*refs):
        weight_refs = refs[count : count + len(weights)]
        outs = refs[-len(shapes) - len(scratch) : -len(scratch)]
        out_refs, x_ref = outs[:halves], refs[-len(scratch)]
        copies = []
        if load:
            sources = refs[count + len(weights) :]
            starts = [
                half_of(True, w) if which == "own" else which * (x.shape[1] // 2)
                for x, which in load
            ]
            copies = fetches(list(zip(sources, starts)), outs[halves:], refs[-1])
        for copy in copies:
            copy.start()
        at = 0
        for ref in refs[:count]:
            x_ref[at : at + ref.shape[0]] = ref[...]
            at += ref.shape[0]

        @pl.loop(0, w // tile)
        def _(j):
            cols = pl.ds(pl.multiple_of(j * tile, tile), tile)
            for i, ref in enumerate(weight_refs):
                out_refs[i // 2][i % 2, :, cols] = jnp.dot(
                    x_ref[...], ref[:, cols], preferred_element_type=F32
                )

        for copy in copies:
            copy.wait()

    return pl.pallas_call(
        body,
        name="gate_up",
        in_specs=[VMEM] * (count + len(weights)) + [ANY] * (len(load) + len(after)),
        out_specs=[VMEM] * len(shapes),
        out_shape=shapes,
        scratch_shapes=scratch,
        **params(3 << 20, KERNEL),
    )(*pieces, *map(in_vmem, weights), *[in_hbm(x) for x, _ in load], *after)


def gated(ours, theirs):
    _, m, w = ours.shape
    tile = min(w, 256)

    def body(a_ref, b_ref, o_ref):
        @pl.loop(0, w // tile)
        def _(j):
            cols = pl.ds(pl.multiple_of(j * tile, tile), tile)
            v = a_ref[0, :, cols] + b_ref[0, :, cols]
            u = a_ref[1, :, cols] + b_ref[1, :, cols]
            o_ref[:, cols] = (v / (1.0 + jnp.exp(-v)) * u).astype(BF16)

    return pl.pallas_call(
        body,
        name="gated",
        in_specs=[VMEM, VMEM],
        out_specs=VMEM,
        out_shape=jax.ShapeDtypeStruct((m, w), BF16),
        **params(2 << 20),
    )(ours, theirs)


def down(halves, weights, outs, after):
    m = sum(h.shape[0] for h, _ in halves)
    w = halves[0][0].shape[1]
    n = weights[0].shape[1]
    tile = 1024
    if any(h.shape[0] % 16 for h, _ in halves):
        halves = [tuple(jnp.concatenate(hs, axis=0) for hs in zip(*halves))]
    count = len(halves)

    def body(*refs):
        weight_refs, h_ref = refs[2 * count : 2 * count + 2], refs[-1]
        out_refs = refs[-1 - len(outs) : -1]
        at = 0
        for i in range(count):
            rows = slice(at, at + refs[2 * i].shape[0])
            at = rows.stop
            h_ref[rows, pl.ds(half_of(True, w), w)] = refs[2 * i][...]
            h_ref[rows, pl.ds(half_of(False, w), w)] = refs[2 * i + 1][...]

        for i, d_ref in enumerate(weight_refs):

            @pl.loop(0, n // tile)
            def _(j):
                here = pl.multiple_of(j * tile, tile)
                out = jnp.dot(
                    h_ref[...], d_ref[:, pl.ds(here, tile)], preferred_element_type=F32
                )
                cols = pl.ds(i * n + here, tile)
                for (at, size, dtype), ref in zip(outs, out_refs):
                    ref[:, cols] = out[at : at + size].astype(dtype)

    return pl.pallas_call(
        body,
        name="down",
        in_specs=[VMEM] * (2 * count + 2) + [ANY] * len(after),
        out_specs=[VMEM] * len(outs),
        out_shape=[
            jax.ShapeDtypeStruct((size, 2 * n), dtype) for _, size, dtype in outs
        ],
        scratch_shapes=[pltpu.VMEM((m, 2 * w), BF16)],
        **params(3 << 20),
    )(*[h for pair in halves for h in pair], *map(in_vmem, weights), *after)


def finish(*parts):
    m, n = parts[0].shape

    def body(*refs):
        o_ref = refs[-1]
        for i in range(2):
            own, first, second = refs[3 * i : 3 * i + 3]
            total = own[...] + first[...].astype(F32) + second[...].astype(F32)
            o_ref[i * m : (i + 1) * m] = total.astype(BF16)

    return pl.pallas_call(
        body,
        name="finish",
        grid=(4,),
        in_specs=[pl.BlockSpec((m, n // 4), lambda j: (0, j))] * 6,
        out_specs=pl.BlockSpec((2 * m, n // 4), lambda j: (0, j)),
        out_shape=jax.ShapeDtypeStruct((2 * m, n), BF16),
        **params(4 << 20),
    )(*parts)


def make_shards(n):
    ring = ring_of(n)
    half = n // 2
    to_right = [(ring[i], ring[(i + 1) % n]) for i in range(n)]
    to_left = [(ring[(i + 1) % n], ring[i]) for i in range(n)]
    swap = [(0, 1), (1, 0)]

    def right(x, name="right"):
        with jax.named_scope(name):
            return lax.ppermute(x, "gy", to_right)

    def left(x, name="left"):
        with jax.named_scope(name):
            return lax.ppermute(x, "gy", to_left)

    def other(x, name="swap"):
        with jax.named_scope(name):
            return lax.ppermute(x, "gx", swap)

    def add(part, block):
        return (part + block.astype(F32)).astype(BF16)

    def shards(tokens, gate_weight, up_weight, down_weight):
        rows = tokens.shape[0]
        cut = rows // 2

        a, b = tokens[:cut], tokens[cut:]
        far_r, far_l = right(a, "farR1"), left(b, "farL1")
        wide = bring([gate_weight], False, [])
        near_r, near_l = right(b, "nearR1"), left(a, "nearL1")
        wide += bring([up_weight], False, wide)
        groups, theirs, ours = [], [], []
        after = wide[-1:]
        for d in range(1, half):
            far_r, far_l = gate(far_r, far_l, after=after, work=GATE)
            held = {("far_r", d): far_r, ("far_l", d): far_l}
            after = [far_r]
            far_r, far_l = right(far_r, f"farR{d + 1}"), left(far_l, f"farL{d + 1}")
            if d == 1:
                waiting = {("own", "a"): a, ("own", "b"): b} | held
                done = after
            elif d == 2:
                ours += gate_up(rows_now, wide[2:], after)
                waiting, done = held, ours[-1:]
            else:
                waiting |= held
                groups.append(list(waiting))
                out = gate_up(list(waiting.values()), wide, after)
                theirs.append(out[0])
                ours.append(out[1])
                waiting, done = {}, out[:1]
            near_r, near_l = gate(near_r, near_l, after=done, work=GATE)
            waiting |= {("near_r", d): near_r, ("near_l", d): near_l}
            after = [near_r]
            if d < half - 1:
                near_r = right(near_r, f"nearR{d + 1}")
                near_l = left(near_l, f"nearL{d + 1}")
            if d == 1:
                groups.append(list(waiting))
                rows_now = list(waiting.values())
                load = [(gate_weight, "own"), (up_weight, "own")]
                out = gate_up(rows_now, wide, after, load)
                theirs.append(out[0])
                wide += out[1:]
                after = out[:1]
        far_r, far_l, *theirs = gate(far_r, far_l, *theirs, after=after)
        waiting |= {("far_r", half): far_r, ("far_l", half): far_l}

        def hide(ours, got):
            h = gated(ours, got)
            return h, other(h)

        last = list(waiting.values())
        last_theirs, low = gate_up(last, wide[:2], [], [(down_weight, 0)])
        last_got = other(last_theirs)
        got = [other(x) for x in theirs]
        last_ours, high = gate_up(last, wide[2:], [last_theirs], [(down_weight, 1)])
        weight = [low, high]
        last = hide(last_ours, last_got)
        outs = [(i * cut, cut, BF16) for i in range(4)]
        b_l, b_r, a_l, a_r = down([last], weight, outs, [])
        hidden = [hide(*pair) for pair in zip(ours, got)]

        def put_down(which, after):
            size = sum(h.shape[0] for h, _ in hidden[which])
            outs = [(0, size, F32)]
            (rest,) = down(hidden[which], weight, outs, after)
            at = 0
            for key in sum(groups[which], []):
                part[key] = rest[at : at + cut]
                at += cut
            return rest

        part = {}
        a_l, a_r = left(a_l), right(a_r)
        b_l, b_r = left(b_l), right(b_r)
        after = [put_down(slice(-1, None), [])]
        for d in range(half - 1, 0, -1):
            a_l, a_r = gate(a_l, a_r, after=after)
            a_l, a_r = add(part["far_r", d], a_l), add(part["far_l", d], a_r)
            after = [a_l, a_r]
            a_l, a_r = left(a_l), right(a_r)
            b_l, b_r = gate(b_l, b_r, after=after)
            if d > 1:
                b_l = add(part["near_r", d - 1], b_l)
                b_r = add(part["near_l", d - 1], b_r)
                after = [b_l, b_r]
                b_l, b_r = left(b_l), right(b_r)
            if d == half - 1:
                after = [put_down(slice(0, -1), after)]
        a_l, a_r = gate(a_l, a_r, after=[b_l])
        return finish(part["own", "a"], a_l, b_r, part["own", "b"], a_r, b_l)

    return shards


def solution(mesh):
    return jax.shard_map(
        make_shards(mesh.shape["gy"]),
        mesh=mesh,
        in_specs=(P(("groups", "gy"), "gx"), P("gx", "gy"), P("gx", "gy"), P("gy", "gx")),
        out_specs=P(("groups", "gy"), "gx"),
        check_vma=False,
    )
```

```python
import jax
import jax.numpy as jnp
from jax import lax
from jax.experimental import pallas as pl
from jax.experimental.pallas import tpu as pltpu
from jax.sharding import PartitionSpec as P

F32, BF16 = jnp.float32, jnp.bfloat16
ANY = pl.BlockSpec(memory_space=pl.ANY)
VMEM = pl.BlockSpec(memory_space=pltpu.VMEM)


def ring_of(n):
    return list(range(0, n, 2)) + list(range(n - 1, 0, -2))


def in_hbm(x):
    return pltpu.with_memory_space_constraint(x, pltpu.HBM)


def in_vmem(x):
    return pltpu.with_memory_space_constraint(x, pltpu.VMEM)


GATE, KERNEL = 22_000_000_000, 1_100_000_000


def params(vmem, work=0):
    return dict(
        compiler_params=pltpu.CompilerParams(vmem_limit_bytes=vmem),
        cost_estimate=pl.CostEstimate(flops=work, bytes_accessed=0, transcendentals=0),
    )


def gate(*arrays, after=(), work=0):
    return pl.pallas_call(
        lambda *refs: None,
        name="gate",
        in_specs=[ANY] * (len(arrays) + len(after)),
        out_specs=[ANY] * len(arrays),
        out_shape=[jax.ShapeDtypeStruct(x.shape, x.dtype) for x in arrays],
        input_output_aliases={i: i for i in range(len(arrays))},
        **params(1 << 18, work),
    )(*arrays, *after)


def fetches(sources, targets, sems, pieces=8):
    copies = []
    for i, ((source, start), target) in enumerate(zip(sources, targets)):
        step = target.shape[0] // pieces
        for s in range(pieces):
            rows = pl.ds(s * step, step)
            cols = pl.ds(start, target.shape[1])
            copies.append(
                pltpu.make_async_copy(
                    source.at[rows, cols], target.at[rows], sems.at[i, s]
                )
            )
    return copies


def half_of(mine, w):
    core = lax.axis_index("gx")
    return pl.multiple_of((core if mine else 1 - core) * w, w)


def bring(weights, mine, after):
    k, w = weights[0].shape[0], weights[0].shape[1] // 2
    count = len(weights)

    def body(*refs):
        sources = [(ref, half_of(mine, w)) for ref in refs[:count]]
        copies = fetches(sources, refs[-1 - count : -1], refs[-1])
        for copy in copies:
            copy.start()
        for copy in copies:
            copy.wait()

    return pl.pallas_call(
        body,
        name="bring",
        in_specs=[ANY] * (count + len(after)),
        out_specs=[VMEM] * count,
        out_shape=[pltpu.VMEM((k, w), weights[0].dtype)] * count,
        scratch_shapes=[pltpu.SemaphoreType.DMA((count, 8))],
        **params(1 << 18, KERNEL),
    )(*map(in_hbm, weights), *after)


def gate_up(pieces, weights, after, load=()):
    if any(p.shape[0] % 16 for p in pieces):
        pieces = [jnp.concatenate(pieces, axis=0)]
    m, k = sum(p.shape[0] for p in pieces), pieces[0].shape[1]
    w = weights[0].shape[1]
    tile = min(w, 512 if load else 1024)
    count, halves = len(pieces), len(weights) // 2
    shapes = [jax.ShapeDtypeStruct((2, m, w), F32)] * halves
    scratch = [pltpu.VMEM((m, k), BF16)]
    for x, _ in load:
        shapes.append(pltpu.VMEM((x.shape[0], x.shape[1] // 2), x.dtype))
    if load:
        scratch.append(pltpu.SemaphoreType.DMA((len(load), 8)))

    def body(*refs):
        weight_refs = refs[count : count + len(weights)]
        outs = refs[-len(shapes) - len(scratch) : -len(scratch)]
        out_refs, x_ref = outs[:halves], refs[-len(scratch)]
        copies = []
        if load:
            sources = refs[count + len(weights) :]
            starts = [
                half_of(True, w) if which == "own" else which * (x.shape[1] // 2)
                for x, which in load
            ]
            copies = fetches(list(zip(sources, starts)), outs[halves:], refs[-1])
        for copy in copies:
            copy.start()
        at = 0
        for ref in refs[:count]:
            x_ref[at : at + ref.shape[0]] = ref[...]
            at += ref.shape[0]

        @pl.loop(0, w // tile)
        def _(j):
            cols = pl.ds(pl.multiple_of(j * tile, tile), tile)
            for i, ref in enumerate(weight_refs):
                out_refs[i // 2][i % 2, :, cols] = jnp.dot(
                    x_ref[...], ref[:, cols], preferred_element_type=F32
                )

        for copy in copies:
            copy.wait()

    return pl.pallas_call(
        body,
        name="gate_up",
        in_specs=[VMEM] * (count + len(weights)) + [ANY] * (len(load) + len(after)),
        out_specs=[VMEM] * len(shapes),
        out_shape=shapes,
        scratch_shapes=scratch,
        **params(3 << 20, KERNEL),
    )(*pieces, *map(in_vmem, weights), *[in_hbm(x) for x, _ in load], *after)


def gated(ours, theirs):
    _, m, w = ours.shape
    tile = min(w, 256)

    def body(a_ref, b_ref, o_ref):
        @pl.loop(0, w // tile)
        def _(j):
            cols = pl.ds(pl.multiple_of(j * tile, tile), tile)
            v = a_ref[0, :, cols] + b_ref[0, :, cols]
            u = a_ref[1, :, cols] + b_ref[1, :, cols]
            o_ref[:, cols] = (v / (1.0 + jnp.exp(-v)) * u).astype(BF16)

    return pl.pallas_call(
        body,
        name="gated",
        in_specs=[VMEM, VMEM],
        out_specs=VMEM,
        out_shape=jax.ShapeDtypeStruct((m, w), BF16),
        **params(2 << 20),
    )(ours, theirs)


def down(halves, weights, outs, after):
    m = sum(h.shape[0] for h, _ in halves)
    w = halves[0][0].shape[1]
    n = weights[0].shape[1]
    tile = 1024
    if any(h.shape[0] % 16 for h, _ in halves):
        halves = [tuple(jnp.concatenate(hs, axis=0) for hs in zip(*halves))]
    count = len(halves)

    def body(*refs):
        weight_refs, h_ref = refs[2 * count : 2 * count + 2], refs[-1]
        out_refs = refs[-1 - len(outs) : -1]
        at = 0
        for i in range(count):
            rows = slice(at, at + refs[2 * i].shape[0])
            at = rows.stop
            h_ref[rows, pl.ds(half_of(True, w), w)] = refs[2 * i][...]
            h_ref[rows, pl.ds(half_of(False, w), w)] = refs[2 * i + 1][...]

        for i, d_ref in enumerate(weight_refs):

            @pl.loop(0, n // tile)
            def _(j):
                here = pl.multiple_of(j * tile, tile)
                out = jnp.dot(
                    h_ref[...], d_ref[:, pl.ds(here, tile)], preferred_element_type=F32
                )
                cols = pl.ds(i * n + here, tile)
                for (at, size, dtype), ref in zip(outs, out_refs):
                    ref[:, cols] = out[at : at + size].astype(dtype)

    return pl.pallas_call(
        body,
        name="down",
        in_specs=[VMEM] * (2 * count + 2) + [ANY] * len(after),
        out_specs=[VMEM] * len(outs),
        out_shape=[
            jax.ShapeDtypeStruct((size, 2 * n), dtype) for _, size, dtype in outs
        ],
        scratch_shapes=[pltpu.VMEM((m, 2 * w), BF16)],
        **params(3 << 20),
    )(*[h for pair in halves for h in pair], *map(in_vmem, weights), *after)


def make_shards(n):
    ring = ring_of(n)
    half = n // 2
    to_right = [(ring[i], ring[(i + 1) % n]) for i in range(n)]
    to_left = [(ring[(i + 1) % n], ring[i]) for i in range(n)]
    swap = [(0, 1), (1, 0)]

    def right(x, name="right"):
        with jax.named_scope(name):
            return lax.ppermute(x, "gy", to_right)

    def left(x, name="left"):
        with jax.named_scope(name):
            return lax.ppermute(x, "gy", to_left)

    def other(x, name="swap"):
        with jax.named_scope(name):
            return lax.ppermute(x, "gx", swap)

    def add(part, block):
        return (part + block.astype(F32)).astype(BF16)

    def shards(tokens, gate_weight, up_weight, down_weight):
        rows = tokens.shape[0]
        cut = rows // 2

        a, b = tokens[:cut], tokens[cut:]
        far_r, far_l = right(a, "farR1"), left(b, "farL1")
        wide = bring([gate_weight], False, [])
        near_r, near_l = right(b, "nearR1"), left(a, "nearL1")
        wide += bring([up_weight], False, wide)
        groups, theirs, ours = [], [], []
        after = wide[-1:]
        for d in range(1, half):
            far_r, far_l = gate(far_r, far_l, after=after, work=GATE)
            held = {("far_r", d): far_r, ("far_l", d): far_l}
            after = [far_r]
            far_r, far_l = right(far_r, f"farR{d + 1}"), left(far_l, f"farL{d + 1}")
            if d == 1:
                waiting = {("own", "a"): a, ("own", "b"): b} | held
                done = after
            elif d == 2:
                ours += gate_up(rows_now, wide[2:], after)
                waiting, done = held, ours[-1:]
            else:
                waiting |= held
                groups.append(list(waiting))
                out = gate_up(list(waiting.values()), wide, after)
                theirs.append(out[0])
                ours.append(out[1])
                waiting, done = {}, out[:1]
            near_r, near_l = gate(near_r, near_l, after=done, work=GATE)
            waiting |= {("near_r", d): near_r, ("near_l", d): near_l}
            after = [near_r]
            if d < half - 1:
                near_r = right(near_r, f"nearR{d + 1}")
                near_l = left(near_l, f"nearL{d + 1}")
            if d == 1:
                groups.append(list(waiting))
                rows_now = list(waiting.values())
                load = [(gate_weight, "own"), (up_weight, "own")]
                out = gate_up(rows_now, wide, after, load)
                theirs.append(out[0])
                wide += out[1:]
                after = out[:1]
        far_r, far_l, *theirs = gate(far_r, far_l, *theirs, after=after)
        waiting |= {("far_r", half): far_r, ("far_l", half): far_l}

        def hide(ours, got):
            h = gated(ours, got)
            return h, other(h)

        last = list(waiting.values())
        last_theirs, low = gate_up(last, wide[:2], [], [(down_weight, 0)])
        last_got = other(last_theirs)
        got = [other(x) for x in theirs]
        last_ours, high = gate_up(last, wide[2:], [last_theirs], [(down_weight, 1)])
        weight = [low, high]
        last = hide(last_ours, last_got)
        outs = [(i * cut, cut, BF16) for i in range(4)]
        b_l, b_r, a_l, a_r = down([last], weight, outs, [])
        hidden = [hide(*pair) for pair in zip(ours, got)]

        def put_down(which, after):
            size = sum(h.shape[0] for h, _ in hidden[which])
            outs = [(0, size, F32)]
            (rest,) = down(hidden[which], weight, outs, after)
            at = 0
            for key in sum(groups[which], []):
                part[key] = rest[at : at + cut]
                at += cut
            return rest

        part = {}
        a_l, a_r = left(a_l), right(a_r)
        b_l, b_r = left(b_l), right(b_r)
        after = [put_down(slice(-1, None), [])]
        for d in range(half - 1, 0, -1):
            a_l, a_r = gate(a_l, a_r, after=after)
            a_l, a_r = add(part["far_r", d], a_l), add(part["far_l", d], a_r)
            after = [a_l, a_r]
            a_l, a_r = left(a_l), right(a_r)
            b_l, b_r = gate(b_l, b_r, after=after)
            if d > 1:
                b_l = add(part["near_r", d - 1], b_l)
                b_r = add(part["near_l", d - 1], b_r)
                after = [b_l, b_r]
                b_l, b_r = left(b_l), right(b_r)
            if d == half - 1:
                after = [put_down(slice(0, -1), after)]
        a_l, a_r = gate(a_l, a_r, after=[b_l])
        total_a = part["own", "a"] + a_l.astype(F32) + b_r.astype(F32)
        total_b = part["own", "b"] + a_r.astype(F32) + b_l.astype(F32)
        return jnp.concatenate([total_a, total_b], axis=0).astype(BF16)

    return shards


def solution(mesh):
    return jax.shard_map(
        make_shards(mesh.shape["gy"]),
        mesh=mesh,
        in_specs=(P(("groups", "gy"), "gx"), P("gx", "gy"), P("gx", "gy"), P("gy", "gx")),
        out_specs=P(("groups", "gy"), "gx"),
        check_vma=False,
    )
```

```python
import jax
import jax.numpy as jnp
from jax import lax
from jax.experimental import pallas as pl
from jax.experimental.pallas import tpu as pltpu
from jax.sharding import PartitionSpec as P

F32, BF16 = jnp.float32, jnp.bfloat16
ANY = pl.BlockSpec(memory_space=pl.ANY)
VMEM = pl.BlockSpec(memory_space=pltpu.VMEM)


def ring_of(n):
    return list(range(0, n, 2)) + list(range(n - 1, 0, -2))


def in_hbm(x):
    return pltpu.with_memory_space_constraint(x, pltpu.HBM)


def in_vmem(x):
    return pltpu.with_memory_space_constraint(x, pltpu.VMEM)


GATE, KERNEL = 22_000_000_000, 1_100_000_000


def params(vmem, work=0):
    return dict(
        compiler_params=pltpu.CompilerParams(vmem_limit_bytes=vmem),
        cost_estimate=pl.CostEstimate(flops=work, bytes_accessed=0, transcendentals=0),
    )


def gate(*arrays, after=(), work=0):
    return pl.pallas_call(
        lambda *refs: None,
        name="gate",
        in_specs=[ANY] * (len(arrays) + len(after)),
        out_specs=[ANY] * len(arrays),
        out_shape=[jax.ShapeDtypeStruct(x.shape, x.dtype) for x in arrays],
        input_output_aliases={i: i for i in range(len(arrays))},
        **params(1 << 18, work),
    )(*arrays, *after)


def fetches(sources, targets, sems, pieces=8):
    copies = []
    for i, ((source, start), target) in enumerate(zip(sources, targets)):
        step = target.shape[0] // pieces
        for s in range(pieces):
            rows = pl.ds(s * step, step)
            cols = pl.ds(start, target.shape[1])
            copies.append(
                pltpu.make_async_copy(
                    source.at[rows, cols], target.at[rows], sems.at[i, s]
                )
            )
    return copies


def half_of(mine, w):
    core = lax.axis_index("gx")
    return pl.multiple_of((core if mine else 1 - core) * w, w)


def bring(weights, mine, after):
    k, w = weights[0].shape[0], weights[0].shape[1] // 2
    count = len(weights)

    def body(*refs):
        sources = [(ref, half_of(mine, w)) for ref in refs[:count]]
        copies = fetches(sources, refs[-1 - count : -1], refs[-1])
        for copy in copies:
            copy.start()
        for copy in copies:
            copy.wait()

    return pl.pallas_call(
        body,
        name="bring",
        in_specs=[ANY] * (count + len(after)),
        out_specs=[VMEM] * count,
        out_shape=[pltpu.VMEM((k, w), weights[0].dtype)] * count,
        scratch_shapes=[pltpu.SemaphoreType.DMA((count, 8))],
        **params(1 << 18, KERNEL),
    )(*map(in_hbm, weights), *after)


def gate_up(pieces, weights, after, load=()):
    if any(p.shape[0] % 16 for p in pieces):
        pieces = [jnp.concatenate(pieces, axis=0)]
    m, k = sum(p.shape[0] for p in pieces), pieces[0].shape[1]
    w = weights[0].shape[1]
    tile = min(w, 512 if load else 1024)
    count, halves = len(pieces), len(weights) // 2
    shapes = [jax.ShapeDtypeStruct((2, m, w), F32)] * halves
    scratch = [pltpu.VMEM((m, k), BF16)]
    for x, cols, _ in load:
        shapes.append(pltpu.VMEM((x.shape[0], cols), x.dtype))
    if load:
        scratch.append(pltpu.SemaphoreType.DMA((len(load), 8)))

    def body(*refs):
        weight_refs = refs[count : count + len(weights)]
        outs = refs[-len(shapes) - len(scratch) : -len(scratch)]
        out_refs, x_ref = outs[:halves], refs[-len(scratch)]
        copies = []
        if load:
            sources = refs[count + len(weights) :]
            starts = [half_of(True, w) if at is None else at for _, _, at in load]
            copies = fetches(list(zip(sources, starts)), outs[halves:], refs[-1])
        for copy in copies:
            copy.start()
        at = 0
        for ref in refs[:count]:
            x_ref[at : at + ref.shape[0]] = ref[...]
            at += ref.shape[0]

        @pl.loop(0, w // tile)
        def _(j):
            cols = pl.ds(pl.multiple_of(j * tile, tile), tile)
            for i, ref in enumerate(weight_refs):
                out_refs[i // 2][i % 2, :, cols] = jnp.dot(
                    x_ref[...], ref[:, cols], preferred_element_type=F32
                )

        for copy in copies:
            copy.wait()

    return pl.pallas_call(
        body,
        name="gate_up",
        in_specs=[VMEM] * (count + len(weights)) + [ANY] * (len(load) + len(after)),
        out_specs=[VMEM] * len(shapes),
        out_shape=shapes,
        scratch_shapes=scratch,
        **params(3 << 20, KERNEL),
    )(*pieces, *map(in_vmem, weights), *[in_hbm(x) for x, _, _ in load], *after)


def gated(ours, theirs):
    _, m, w = ours.shape
    tile = min(w, 256)

    def body(a_ref, b_ref, o_ref):
        @pl.loop(0, w // tile)
        def _(j):
            cols = pl.ds(pl.multiple_of(j * tile, tile), tile)
            v = a_ref[0, :, cols] + b_ref[0, :, cols]
            u = a_ref[1, :, cols] + b_ref[1, :, cols]
            o_ref[:, cols] = (v / (1.0 + jnp.exp(-v)) * u).astype(BF16)

    return pl.pallas_call(
        body,
        name="gated",
        in_specs=[VMEM, VMEM],
        out_specs=VMEM,
        out_shape=jax.ShapeDtypeStruct((m, w), BF16),
        **params(2 << 20),
    )(ours, theirs)


def down(halves, weights, outs, after):
    *weights, whole = weights
    m = sum(h.shape[0] for h, _ in halves)
    w = halves[0][0].shape[1]
    n, wide = whole.shape[1], weights[0].shape[1]
    rest = n - 2 * wide
    tile = wide // 2
    if any(h.shape[0] % 16 for h, _ in halves):
        halves = [tuple(jnp.concatenate(hs, axis=0) for hs in zip(*halves))]
    count = len(halves)

    def body(*refs):
        weight_refs, source = refs[2 * count : 2 * count + 2], refs[2 * count + 2]
        out_refs, (h_ref, rest_ref, sems) = refs[-3 - len(outs) : -3], refs[-3:]
        copies = fetches([(source, 2 * wide)], [rest_ref], sems)
        for copy in copies:
            copy.start()
        at = 0
        for i in range(count):
            rows = slice(at, at + refs[2 * i].shape[0])
            at = rows.stop
            h_ref[rows, pl.ds(half_of(True, w), w)] = refs[2 * i][...]
            h_ref[rows, pl.ds(half_of(False, w), w)] = refs[2 * i + 1][...]

        def multiply(columns, cols):
            out = jnp.dot(h_ref[...], columns, preferred_element_type=F32)
            for (at, size, dtype), ref in zip(outs, out_refs):
                ref[:, cols] = out[at : at + size].astype(dtype)

        for i, d_ref in enumerate(weight_refs):

            @pl.loop(0, 2)
            def _(j):
                here = pl.multiple_of(j * tile, tile)
                multiply(d_ref[:, pl.ds(here, tile)], pl.ds(i * wide + here, tile))

        for copy in copies:
            copy.wait()
        multiply(rest_ref[...], pl.ds(2 * wide, rest))

    return pl.pallas_call(
        body,
        name="down",
        in_specs=[VMEM] * (2 * count + 2) + [ANY] * (1 + len(after)),
        out_specs=[VMEM] * len(outs),
        out_shape=[jax.ShapeDtypeStruct((size, n), dtype) for _, size, dtype in outs],
        scratch_shapes=[
            pltpu.VMEM((m, 2 * w), BF16),
            pltpu.VMEM((2 * w, rest), BF16),
            pltpu.SemaphoreType.DMA((1, 8)),
        ],
        **params(8 << 20),
    )(
        *[h for pair in halves for h in pair],
        *map(in_vmem, weights),
        in_hbm(whole),
        *after,
    )


def make_shards(n):
    ring = ring_of(n)
    half = n // 2
    to_right = [(ring[i], ring[(i + 1) % n]) for i in range(n)]
    to_left = [(ring[(i + 1) % n], ring[i]) for i in range(n)]
    swap = [(0, 1), (1, 0)]

    def right(x, name="right"):
        with jax.named_scope(name):
            return lax.ppermute(x, "gy", to_right)

    def left(x, name="left"):
        with jax.named_scope(name):
            return lax.ppermute(x, "gy", to_left)

    def other(x, name="swap"):
        with jax.named_scope(name):
            return lax.ppermute(x, "gx", swap)

    def add(part, block):
        return (part + block.astype(F32)).astype(BF16)

    def shards(tokens, gate_weight, up_weight, down_weight):
        rows = tokens.shape[0]
        cut = rows // 2

        a, b = tokens[:cut], tokens[cut:]
        far_r, far_l = right(a, "farR1"), left(b, "farL1")
        wide = bring([gate_weight], False, [])
        near_r, near_l = right(b, "nearR1"), left(a, "nearL1")
        wide += bring([up_weight], False, wide)
        groups, theirs, ours = [], [], []
        after = wide[-1:]
        for d in range(1, half):
            far_r, far_l = gate(far_r, far_l, after=after, work=GATE)
            held = {("far_r", d): far_r, ("far_l", d): far_l}
            after = [far_r]
            far_r, far_l = right(far_r, f"farR{d + 1}"), left(far_l, f"farL{d + 1}")
            if d == 1:
                waiting = {("own", "a"): a, ("own", "b"): b} | held
                done = after
            elif d == 2:
                ours += gate_up(rows_now, wide[2:], after)
                waiting, done = held, ours[-1:]
            else:
                waiting |= held
                groups.append(list(waiting))
                out = gate_up(list(waiting.values()), wide, after)
                theirs.append(out[0])
                ours.append(out[1])
                waiting, done = {}, out[:1]
            near_r, near_l = gate(near_r, near_l, after=done, work=GATE)
            waiting |= {("near_r", d): near_r, ("near_l", d): near_l}
            after = [near_r]
            if d < half - 1:
                near_r = right(near_r, f"nearR{d + 1}")
                near_l = left(near_l, f"nearL{d + 1}")
            if d == 1:
                groups.append(list(waiting))
                rows_now = list(waiting.values())
                load = [(x, x.shape[1] // 2, None) for x in (gate_weight, up_weight)]
                out = gate_up(rows_now, wide, after, load)
                theirs.append(out[0])
                wide += out[1:]
                after = out[:1]
        far_r, far_l, *theirs = gate(far_r, far_l, *theirs, after=after)
        waiting |= {("far_r", half): far_r, ("far_l", half): far_l}

        def hide(ours, got):
            h = gated(ours, got)
            return h, other(h)

        last = list(waiting.values())
        part_cols = down_weight.shape[1] * 3 // 8
        load = [(down_weight, part_cols, 0)]
        last_theirs, low = gate_up(last, wide[:2], [], load)
        last_got = other(last_theirs)
        got = [other(x) for x in theirs]
        load = [(down_weight, part_cols, part_cols)]
        last_ours, high = gate_up(last, wide[2:], [last_theirs], load)
        weight = [low, high, down_weight]
        last = hide(last_ours, last_got)
        outs = [(i * cut, cut, BF16) for i in range(4)]
        b_l, b_r, a_l, a_r = down([last], weight, outs, [])
        hidden = [hide(*pair) for pair in zip(ours, got)]

        def put_down(which, after):
            size = sum(h.shape[0] for h, _ in hidden[which])
            outs = [(0, size, F32)]
            (rest,) = down(hidden[which], weight, outs, after)
            at = 0
            for key in sum(groups[which], []):
                part[key] = rest[at : at + cut]
                at += cut
            return rest

        part = {}
        a_l, a_r = left(a_l), right(a_r)
        b_l, b_r = left(b_l), right(b_r)
        after = [put_down(slice(-1, None), [])]
        for d in range(half - 1, 0, -1):
            a_l, a_r = gate(a_l, a_r, after=after)
            a_l, a_r = add(part["far_r", d], a_l), add(part["far_l", d], a_r)
            after = [a_l, a_r]
            a_l, a_r = left(a_l), right(a_r)
            b_l, b_r = gate(b_l, b_r, after=after)
            if d > 1:
                b_l = add(part["near_r", d - 1], b_l)
                b_r = add(part["near_l", d - 1], b_r)
                after = [b_l, b_r]
                b_l, b_r = left(b_l), right(b_r)
            if d == half - 1:
                after = [put_down(slice(0, -1), after)]
        a_l, a_r = gate(a_l, a_r, after=[b_l])
        total_a = part["own", "a"] + a_l.astype(F32) + b_r.astype(F32)
        total_b = part["own", "b"] + a_r.astype(F32) + b_l.astype(F32)
        return jnp.concatenate([total_a, total_b], axis=0).astype(BF16)

    return shards


def solution(mesh):
    return jax.shard_map(
        make_shards(mesh.shape["gy"]),
        mesh=mesh,
        in_specs=(P(("groups", "gy"), "gx"), P("gx", "gy"), P("gx", "gy"), P("gy", "gx")),
        out_specs=P(("groups", "gy"), "gx"),
        check_vma=False,
    )
```

```python
import jax
import jax.numpy as jnp
from jax import lax
from jax.experimental import pallas as pl
from jax.experimental.pallas import tpu as pltpu
from jax.sharding import PartitionSpec as P

F32, BF16 = jnp.float32, jnp.bfloat16
ANY = pl.BlockSpec(memory_space=pl.ANY)
VMEM = pl.BlockSpec(memory_space=pltpu.VMEM)


def ring_of(n):
    return list(range(0, n, 2)) + list(range(n - 1, 0, -2))


def in_hbm(x):
    return pltpu.with_memory_space_constraint(x, pltpu.HBM)


def in_vmem(x):
    return pltpu.with_memory_space_constraint(x, pltpu.VMEM)


GATE, KERNEL = 22_000_000_000, 1_100_000_000


def params(vmem, work=0):
    return dict(
        compiler_params=pltpu.CompilerParams(vmem_limit_bytes=vmem),
        cost_estimate=pl.CostEstimate(flops=work, bytes_accessed=0, transcendentals=0),
    )


def gate(*arrays, after=(), work=0):
    return pl.pallas_call(
        lambda *refs: None,
        name="gate",
        in_specs=[ANY] * (len(arrays) + len(after)),
        out_specs=[ANY] * len(arrays),
        out_shape=[jax.ShapeDtypeStruct(x.shape, x.dtype) for x in arrays],
        input_output_aliases={i: i for i in range(len(arrays))},
        **params(1 << 18, work),
    )(*arrays, *after)


def fetches(sources, targets, sems, pieces=8):
    copies = []
    for i, ((source, start), target) in enumerate(zip(sources, targets)):
        step = target.shape[0] // pieces
        for s in range(pieces):
            rows = pl.ds(s * step, step)
            cols = pl.ds(start, target.shape[1])
            copies.append(
                pltpu.make_async_copy(
                    source.at[rows, cols], target.at[rows], sems.at[i, s]
                )
            )
    return copies


def half_of(mine, w):
    core = lax.axis_index("gx")
    return pl.multiple_of((core if mine else 1 - core) * w, w)


def bring(weights, mine, after):
    k, w = weights[0].shape[0], weights[0].shape[1] // 2
    count = len(weights)

    def body(*refs):
        sources = [(ref, half_of(mine, w)) for ref in refs[:count]]
        copies = fetches(sources, refs[-1 - count : -1], refs[-1])
        for copy in copies:
            copy.start()
        for copy in copies:
            copy.wait()

    return pl.pallas_call(
        body,
        name="bring",
        in_specs=[ANY] * (count + len(after)),
        out_specs=[VMEM] * count,
        out_shape=[pltpu.VMEM((k, w), weights[0].dtype)] * count,
        scratch_shapes=[pltpu.SemaphoreType.DMA((count, 8))],
        **params(1 << 18, KERNEL),
    )(*map(in_hbm, weights), *after)


def gate_up(pieces, weights, after, load=()):
    if any(p.shape[0] % 16 for p in pieces):
        pieces = [jnp.concatenate(pieces, axis=0)]
    m, k = sum(p.shape[0] for p in pieces), pieces[0].shape[1]
    w = weights[0].shape[1]
    tile = min(w, 512 if load else 1024)
    count, halves = len(pieces), len(weights) // 2
    shapes = [jax.ShapeDtypeStruct((2, m, w), F32)] * halves
    scratch = [pltpu.VMEM((m, k), BF16)]
    for x, cols, _ in load:
        shapes.append(pltpu.VMEM((x.shape[0], cols), x.dtype))
    if load:
        scratch.append(pltpu.SemaphoreType.DMA((len(load), 8)))

    def body(*refs):
        weight_refs = refs[count : count + len(weights)]
        outs = refs[-len(shapes) - len(scratch) : -len(scratch)]
        out_refs, x_ref = outs[:halves], refs[-len(scratch)]
        copies = []
        if load:
            sources = refs[count + len(weights) :]
            starts = [half_of(True, w) if at is None else at for _, _, at in load]
            copies = fetches(list(zip(sources, starts)), outs[halves:], refs[-1])
        for copy in copies:
            copy.start()
        at = 0
        for ref in refs[:count]:
            x_ref[at : at + ref.shape[0]] = ref[...]
            at += ref.shape[0]

        @pl.loop(0, w // tile)
        def _(j):
            cols = pl.ds(pl.multiple_of(j * tile, tile), tile)
            for i, ref in enumerate(weight_refs):
                out_refs[i // 2][i % 2, :, cols] = jnp.dot(
                    x_ref[...], ref[:, cols], preferred_element_type=F32
                )

        for copy in copies:
            copy.wait()

    return pl.pallas_call(
        body,
        name="gate_up",
        in_specs=[VMEM] * (count + len(weights)) + [ANY] * (len(load) + len(after)),
        out_specs=[VMEM] * len(shapes),
        out_shape=shapes,
        scratch_shapes=scratch,
        **params(3 << 20, KERNEL),
    )(*pieces, *map(in_vmem, weights), *[in_hbm(x) for x, _, _ in load], *after)


def gated(ours, *theirs):
    m, w = sum(size for _, size, _ in theirs), ours.shape[2]
    tile = min(w, 256)

    def body(a_ref, *refs):
        o_ref = refs[-1]

        @pl.loop(0, w // tile)
        def _(j):
            cols = pl.ds(pl.multiple_of(j * tile, tile), tile)
            at = 0
            for b_ref, (_, size, first) in zip(refs, theirs):
                mine, others = pl.ds(at, size), pl.ds(first, size)
                v = a_ref[0, mine, cols] + b_ref[0, others, cols]
                u = a_ref[1, mine, cols] + b_ref[1, others, cols]
                o_ref[mine, cols] = (v / (1.0 + jnp.exp(-v)) * u).astype(BF16)
                at += size

    return pl.pallas_call(
        body,
        name="gated",
        in_specs=[VMEM] * (1 + len(theirs)),
        out_specs=VMEM,
        out_shape=jax.ShapeDtypeStruct((m, w), BF16),
        **params(2 << 20),
    )(ours, *[x for x, _, _ in theirs])


def down(halves, weights, outs, after):
    *weights, whole = weights
    m = sum(h.shape[0] for h, _ in halves)
    w = halves[0][0].shape[1]
    n, wide = whole.shape[1], weights[0].shape[1]
    rest = n - 2 * wide
    tile = wide // 2
    if any(h.shape[0] % 16 for h, _ in halves):
        halves = [tuple(jnp.concatenate(hs, axis=0) for hs in zip(*halves))]
    count = len(halves)

    def body(*refs):
        weight_refs, source = refs[2 * count : 2 * count + 2], refs[2 * count + 2]
        out_refs, (h_ref, rest_ref, sems) = refs[-3 - len(outs) : -3], refs[-3:]
        copies = fetches([(source, 2 * wide)], [rest_ref], sems)
        for copy in copies:
            copy.start()
        at = 0
        for i in range(count):
            rows = slice(at, at + refs[2 * i].shape[0])
            at = rows.stop
            h_ref[rows, pl.ds(half_of(True, w), w)] = refs[2 * i][...]
            h_ref[rows, pl.ds(half_of(False, w), w)] = refs[2 * i + 1][...]

        def multiply(columns, cols):
            out = jnp.dot(h_ref[...], columns, preferred_element_type=F32)
            for (at, size, dtype), ref in zip(outs, out_refs):
                ref[:, cols] = out[at : at + size].astype(dtype)

        for i, d_ref in enumerate(weight_refs):

            @pl.loop(0, 2)
            def _(j):
                here = pl.multiple_of(j * tile, tile)
                multiply(d_ref[:, pl.ds(here, tile)], pl.ds(i * wide + here, tile))

        for copy in copies:
            copy.wait()
        multiply(rest_ref[...], pl.ds(2 * wide, rest))

    return pl.pallas_call(
        body,
        name="down",
        in_specs=[VMEM] * (2 * count + 2) + [ANY] * (1 + len(after)),
        out_specs=[VMEM] * len(outs),
        out_shape=[jax.ShapeDtypeStruct((size, n), dtype) for _, size, dtype in outs],
        scratch_shapes=[
            pltpu.VMEM((m, 2 * w), BF16),
            pltpu.VMEM((2 * w, rest), BF16),
            pltpu.SemaphoreType.DMA((1, 8)),
        ],
        **params(8 << 20),
    )(
        *[h for pair in halves for h in pair],
        *map(in_vmem, weights),
        in_hbm(whole),
        *after,
    )


def make_shards(n):
    ring = ring_of(n)
    half = n // 2
    to_right = [(ring[i], ring[(i + 1) % n]) for i in range(n)]
    to_left = [(ring[(i + 1) % n], ring[i]) for i in range(n)]
    swap = [(0, 1), (1, 0)]

    def right(x, name="right"):
        with jax.named_scope(name):
            return lax.ppermute(x, "gy", to_right)

    def left(x, name="left"):
        with jax.named_scope(name):
            return lax.ppermute(x, "gy", to_left)

    def other(x, name="swap"):
        with jax.named_scope(name):
            return lax.ppermute(x, "gx", swap)

    def add(part, block):
        return (part + block.astype(F32)).astype(BF16)

    def shards(tokens, gate_weight, up_weight, down_weight):
        rows = tokens.shape[0]
        cut = rows // 2

        a, b = tokens[:cut], tokens[cut:]
        far_r, far_l = right(a, "farR1"), left(b, "farL1")
        wide = bring([gate_weight], False, [])
        near_r, near_l = right(b, "nearR1"), left(a, "nearL1")
        wide += bring([up_weight], False, wide)
        groups, theirs, ours = [], [], []
        after = wide[-1:]
        for d in range(1, half):
            far_r, far_l = gate(far_r, far_l, after=after, work=GATE)
            held = {("far_r", d): far_r, ("far_l", d): far_l}
            after = [far_r]
            far_r, far_l = right(far_r, f"farR{d + 1}"), left(far_l, f"farL{d + 1}")
            if d == 1:
                waiting = {("own", "a"): a, ("own", "b"): b} | held
                done = after
            elif d == 2:
                ours += gate_up(rows_now, wide[2:], after)
                waiting, done = held, ours[-1:]
            elif d < half - 1:
                waiting |= held
                groups.append(list(waiting))
                out = gate_up(list(waiting.values()), wide, after)
                theirs.append(out[0])
                ours.append(out[1])
                waiting, done = {}, out[:1]
            else:
                late = list(held.values())
                groups.append(list(waiting | held))
                ours += gate_up(list((waiting | held).values()), wide[2:], after)
                waiting, done = {}, ours[-1:]
            near_r, near_l = gate(near_r, near_l, after=done, work=GATE)
            waiting |= {("near_r", d): near_r, ("near_l", d): near_l}
            after = [near_r]
            if d < half - 1:
                near_r = right(near_r, f"nearR{d + 1}")
                near_l = left(near_l, f"nearL{d + 1}")
            if d == 1:
                groups.append(list(waiting))
                rows_now = list(waiting.values())
                load = [(x, x.shape[1] // 2, None) for x in (gate_weight, up_weight)]
                out = gate_up(rows_now, wide, after, load)
                theirs.append(out[0])
                wide += out[1:]
                after = out[:1]
            if d == half - 2:
                theirs += gate_up(list(waiting.values()), wide[:2], after)
                after = theirs[-1:]
        far_r, far_l, *theirs = gate(far_r, far_l, *theirs, after=after)
        waiting |= {("far_r", half): far_r, ("far_l", half): far_l}

        def hide(*sums):
            h = gated(*sums)
            return h, other(h)

        last = list(waiting.values())
        part_cols = down_weight.shape[1] * 3 // 8
        load = [(down_weight, part_cols, 0)]
        last_theirs, low = gate_up(last + late, wide[:2], [], load)
        last_got = other(last_theirs)
        got = [other(x) for x in theirs]
        load = [(down_weight, part_cols, part_cols)]
        last_ours, high = gate_up(last, wide[2:], [last_theirs], load)
        weight = [low, high, down_weight]
        size = last_ours.shape[1]
        last = hide(last_ours, (last_got, size, 0))
        outs = [(i * cut, cut, BF16) for i in range(4)]
        b_l, b_r, a_l, a_r = down([last], weight, outs, [])
        taken = [[(x, x.shape[1], 0)] for x in got]
        taken[-1].append((last_got, sum(x.shape[0] for x in late), size))
        hidden = [hide(x, *parts) for x, parts in zip(ours, taken)]

        def put_down(which, after):
            outs = [(0, sum(h.shape[0] for h, _ in hidden[which]), F32)]
            (rest,) = down(hidden[which], weight, outs, after)
            at = 0
            for key in sum(groups[which], []):
                part[key] = rest[at : at + cut]
                at += cut
            return rest

        part = {}
        a_l, a_r = left(a_l), right(a_r)
        b_l, b_r = left(b_l), right(b_r)
        after = [put_down(slice(-1, None), [])]
        for d in range(half - 1, 0, -1):
            a_l, a_r = gate(a_l, a_r, after=after)
            a_l, a_r = add(part["far_r", d], a_l), add(part["far_l", d], a_r)
            after = [a_l, a_r]
            a_l, a_r = left(a_l), right(a_r)
            b_l, b_r = gate(b_l, b_r, after=after)
            if d > 1:
                b_l = add(part["near_r", d - 1], b_l)
                b_r = add(part["near_l", d - 1], b_r)
                after = [b_l, b_r]
                b_l, b_r = left(b_l), right(b_r)
            if d == half - 1:
                after = [put_down(slice(0, -1), after)]
        a_l, a_r = gate(a_l, a_r, after=[b_l])
        total_a = part["own", "a"] + a_l.astype(F32) + b_r.astype(F32)
        total_b = part["own", "b"] + a_r.astype(F32) + b_l.astype(F32)
        return jnp.concatenate([total_a, total_b], axis=0).astype(BF16)

    return shards


def solution(mesh):
    return jax.shard_map(
        make_shards(mesh.shape["gy"]),
        mesh=mesh,
        in_specs=(P(("groups", "gy"), "gx"), P("gx", "gy"), P("gx", "gy"), P("gy", "gx")),
        out_specs=P(("groups", "gy"), "gx"),
        check_vma=False,
    )
```

```python
import jax
import jax.numpy as jnp
from jax import lax
from jax.experimental import pallas as pl
from jax.experimental.pallas import tpu as pltpu
from jax.sharding import PartitionSpec as P

F32, BF16 = jnp.float32, jnp.bfloat16
ANY = pl.BlockSpec(memory_space=pl.ANY)
VMEM = pl.BlockSpec(memory_space=pltpu.VMEM)


def ring_of(n):
    return list(range(0, n, 2)) + list(range(n - 1, 0, -2))


def in_hbm(x):
    return pltpu.with_memory_space_constraint(x, pltpu.HBM)


def in_vmem(x):
    return pltpu.with_memory_space_constraint(x, pltpu.VMEM)


GATE, KERNEL = 22_000_000_000, 1_100_000_000


def params(vmem, work=0):
    return dict(
        compiler_params=pltpu.CompilerParams(vmem_limit_bytes=vmem),
        cost_estimate=pl.CostEstimate(flops=work, bytes_accessed=0, transcendentals=0),
    )


def gate(*arrays, after=(), work=0):
    return pl.pallas_call(
        lambda *refs: None,
        name="gate",
        in_specs=[ANY] * (len(arrays) + len(after)),
        out_specs=[ANY] * len(arrays),
        out_shape=[jax.ShapeDtypeStruct(x.shape, x.dtype) for x in arrays],
        input_output_aliases={i: i for i in range(len(arrays))},
        **params(1 << 18, work),
    )(*arrays, *after)


def fetches(sources, targets, sems, pieces=8):
    copies = []
    for i, ((source, start), target) in enumerate(zip(sources, targets)):
        step = target.shape[0] // pieces
        for s in range(pieces):
            rows = pl.ds(s * step, step)
            cols = pl.ds(start, target.shape[1])
            copies.append(
                pltpu.make_async_copy(
                    source.at[rows, cols], target.at[rows], sems.at[i, s]
                )
            )
    return copies


def half_of(mine, w):
    core = lax.axis_index("gx")
    return pl.multiple_of((core if mine else 1 - core) * w, w)


def bring(weights, mine, after):
    k, w = weights[0].shape[0], weights[0].shape[1] // 2
    count = len(weights)

    def body(*refs):
        sources = [(ref, half_of(mine, w)) for ref in refs[:count]]
        copies = fetches(sources, refs[-1 - count : -1], refs[-1])
        for copy in copies:
            copy.start()
        for copy in copies:
            copy.wait()

    return pl.pallas_call(
        body,
        name="bring",
        in_specs=[ANY] * (count + len(after)),
        out_specs=[VMEM] * count,
        out_shape=[pltpu.VMEM((k, w), weights[0].dtype)] * count,
        scratch_shapes=[pltpu.SemaphoreType.DMA((count, 8))],
        **params(1 << 18, KERNEL),
    )(*map(in_hbm, weights), *after)


def gate_up(pieces, weights, after, load=()):
    if any(p.shape[0] % 16 for p in pieces):
        pieces = [jnp.concatenate(pieces, axis=0)]
    m, k = sum(p.shape[0] for p in pieces), pieces[0].shape[1]
    w = weights[0].shape[1]
    tile = min(w, 512 if load else 1024)
    count, halves = len(pieces), len(weights) // 2
    shapes = [jax.ShapeDtypeStruct((2, m, w), F32)] * halves
    scratch = [pltpu.VMEM((m, k), BF16)]
    for x, cols, _ in load:
        shapes.append(pltpu.VMEM((x.shape[0], cols), x.dtype))
    if load:
        scratch.append(pltpu.SemaphoreType.DMA((len(load), 8)))

    def body(*refs):
        weight_refs = refs[count : count + len(weights)]
        outs = refs[-len(shapes) - len(scratch) : -len(scratch)]
        out_refs, x_ref = outs[:halves], refs[-len(scratch)]
        copies = []
        if load:
            sources = refs[count + len(weights) :]
            starts = [half_of(True, w) if at is None else at for _, _, at in load]
            copies = fetches(list(zip(sources, starts)), outs[halves:], refs[-1])
        for copy in copies:
            copy.start()
        at = 0
        for ref in refs[:count]:
            x_ref[at : at + ref.shape[0]] = ref[...]
            at += ref.shape[0]

        @pl.loop(0, w // tile)
        def _(j):
            cols = pl.ds(pl.multiple_of(j * tile, tile), tile)
            for i, ref in enumerate(weight_refs):
                out_refs[i // 2][i % 2, :, cols] = jnp.dot(
                    x_ref[...], ref[:, cols], preferred_element_type=F32
                )

        for copy in copies:
            copy.wait()

    return pl.pallas_call(
        body,
        name="gate_up",
        in_specs=[VMEM] * (count + len(weights)) + [ANY] * (len(load) + len(after)),
        out_specs=[VMEM] * len(shapes),
        out_shape=shapes,
        scratch_shapes=scratch,
        **params(3 << 20, KERNEL),
    )(*pieces, *map(in_vmem, weights), *[in_hbm(x) for x, _, _ in load], *after)


def gated(ours, theirs):
    _, m, w = ours.shape
    tile = min(w, 256)

    def body(a_ref, b_ref, o_ref):
        @pl.loop(0, w // tile)
        def _(j):
            cols = pl.ds(pl.multiple_of(j * tile, tile), tile)
            v = a_ref[0, :, cols] + b_ref[0, :, cols]
            u = a_ref[1, :, cols] + b_ref[1, :, cols]
            o_ref[:, cols] = (v / (1.0 + jnp.exp(-v)) * u).astype(BF16)

    return pl.pallas_call(
        body,
        name="gated",
        in_specs=[VMEM, VMEM],
        out_specs=VMEM,
        out_shape=jax.ShapeDtypeStruct((m, w), BF16),
        **params(2 << 20),
    )(ours, theirs)


def down(halves, weights, outs, after):
    *weights, whole = weights
    m = sum(h.shape[0] for h, _ in halves)
    w = halves[0][0].shape[1]
    n, wide = whole.shape[1], weights[0].shape[1]
    rest = n - 2 * wide
    tile = wide // 2
    if any(h.shape[0] % 16 for h, _ in halves):
        halves = [tuple(jnp.concatenate(hs, axis=0) for hs in zip(*halves))]
    count = len(halves)

    def body(*refs):
        weight_refs, source = refs[2 * count : 2 * count + 2], refs[2 * count + 2]
        out_refs, (h_ref, rest_ref, sems) = refs[-3 - len(outs) : -3], refs[-3:]
        copies = fetches([(source, 2 * wide)], [rest_ref], sems)
        for copy in copies:
            copy.start()
        at = 0
        for i in range(count):
            rows = slice(at, at + refs[2 * i].shape[0])
            at = rows.stop
            h_ref[rows, pl.ds(half_of(True, w), w)] = refs[2 * i][...]
            h_ref[rows, pl.ds(half_of(False, w), w)] = refs[2 * i + 1][...]

        def multiply(columns, cols):
            out = jnp.dot(h_ref[...], columns, preferred_element_type=F32)
            for (at, size, dtype), ref in zip(outs, out_refs):
                ref[:, cols] = out[at : at + size].astype(dtype)

        for i, d_ref in enumerate(weight_refs):

            @pl.loop(0, 2)
            def _(j):
                here = pl.multiple_of(j * tile, tile)
                multiply(d_ref[:, pl.ds(here, tile)], pl.ds(i * wide + here, tile))

        for copy in copies:
            copy.wait()
        multiply(rest_ref[...], pl.ds(2 * wide, rest))

    return pl.pallas_call(
        body,
        name="down",
        in_specs=[VMEM] * (2 * count + 2) + [ANY] * (1 + len(after)),
        out_specs=[VMEM] * len(outs),
        out_shape=[jax.ShapeDtypeStruct((size, n), dtype) for _, size, dtype in outs],
        scratch_shapes=[
            pltpu.VMEM((m, 2 * w), BF16),
            pltpu.VMEM((2 * w, rest), BF16),
            pltpu.SemaphoreType.DMA((1, 8)),
        ],
        **params(8 << 20),
    )(
        *[h for pair in halves for h in pair],
        *map(in_vmem, weights),
        in_hbm(whole),
        *after,
    )


def make_shards(n):
    ring = ring_of(n)
    half = n // 2
    to_right = [(ring[i], ring[(i + 1) % n]) for i in range(n)]
    to_left = [(ring[(i + 1) % n], ring[i]) for i in range(n)]
    swap = [(0, 1), (1, 0)]

    def right(x, name="right"):
        with jax.named_scope(name):
            return lax.ppermute(x, "gy", to_right)

    def left(x, name="left"):
        with jax.named_scope(name):
            return lax.ppermute(x, "gy", to_left)

    def other(x, name="swap"):
        with jax.named_scope(name):
            return lax.ppermute(x, "gx", swap)

    def add(part, block):
        return (part + block.astype(F32)).astype(BF16)

    def shards(tokens, gate_weight, up_weight, down_weight):
        rows = tokens.shape[0]
        cut = rows // 2

        a, b = tokens[:cut], tokens[cut:]
        far_r, far_l = right(a, "farR1"), left(b, "farL1")
        wide = bring([gate_weight], False, [])
        near_r, near_l = right(b, "nearR1"), left(a, "nearL1")
        wide += bring([up_weight], False, wide)
        groups, theirs, ours = [], [], []
        after = wide[-1:]
        for d in range(1, half):
            far_r, far_l = gate(far_r, far_l, after=after, work=GATE)
            held = {("far_r", d): far_r, ("far_l", d): far_l}
            after = [far_r]
            far_r, far_l = right(far_r, f"farR{d + 1}"), left(far_l, f"farL{d + 1}")
            if d == 1:
                waiting = {("own", "a"): a, ("own", "b"): b} | held
                done = after
            elif d == 2:
                ours += gate_up(rows_now, wide[2:], after)
                waiting, done = held, ours[-1:]
            else:
                waiting |= held
                groups.append(list(waiting))
                out = gate_up(list(waiting.values()), wide, after)
                theirs.append(out[0])
                ours.append(out[1])
                waiting, done = {}, out[:1]
            near_r, near_l = gate(near_r, near_l, after=done, work=GATE)
            waiting |= {("near_r", d): near_r, ("near_l", d): near_l}
            after = [near_r]
            if d < half - 1:
                near_r = right(near_r, f"nearR{d + 1}")
                near_l = left(near_l, f"nearL{d + 1}")
            if d == 1:
                groups.append(list(waiting))
                rows_now = list(waiting.values())
                load = [(x, x.shape[1] // 2, None) for x in (gate_weight, up_weight)]
                out = gate_up(rows_now, wide, after, load)
                theirs.append(out[0])
                wide += out[1:]
                after = out[:1]
        far_r, far_l, *theirs = gate(far_r, far_l, *theirs, after=after)
        waiting |= {("far_r", half): far_r, ("far_l", half): far_l}

        def hide(ours, got):
            h = gated(ours, got)
            return h, other(h)

        last = list(waiting.values())
        part_cols = down_weight.shape[1] * 3 // 8
        load = [(down_weight, part_cols, 0)]
        last_theirs, low = gate_up(last, wide[:2], [], load)
        last_got = other(last_theirs)
        got = [other(x) for x in gate(*theirs, after=[last_theirs])]
        load = [(down_weight, part_cols, part_cols)]
        last_ours, high = gate_up(last, wide[2:], [last_theirs], load)
        weight = [low, high, down_weight]
        last = hide(last_ours, last_got)
        outs = [(i * cut, cut, BF16) for i in range(4)]
        b_l, b_r, a_l, a_r = down([last], weight, outs, [])
        hidden = [hide(*pair) for pair in zip(ours, got)]

        def put_down(which, after):
            size = sum(h.shape[0] for h, _ in hidden[which])
            outs = [(0, size, F32)]
            (rest,) = down(hidden[which], weight, outs, after)
            at = 0
            for key in sum(groups[which], []):
                part[key] = rest[at : at + cut]
                at += cut
            return rest

        part = {}
        a_l, a_r = left(a_l), right(a_r)
        b_l, b_r = left(b_l), right(b_r)
        after = [put_down(slice(-1, None), [])]
        for d in range(half - 1, 0, -1):
            a_l, a_r = gate(a_l, a_r, after=after)
            a_l, a_r = add(part["far_r", d], a_l), add(part["far_l", d], a_r)
            after = [a_l, a_r]
            a_l, a_r = left(a_l), right(a_r)
            b_l, b_r = gate(b_l, b_r, after=after)
            if d > 1:
                b_l = add(part["near_r", d - 1], b_l)
                b_r = add(part["near_l", d - 1], b_r)
                after = [b_l, b_r]
                b_l, b_r = left(b_l), right(b_r)
            if d == half - 1:
                after = [put_down(slice(0, -1), after)]
        a_l, a_r = gate(a_l, a_r, after=[b_l])
        total_a = part["own", "a"] + a_l.astype(F32) + b_r.astype(F32)
        total_b = part["own", "b"] + a_r.astype(F32) + b_l.astype(F32)
        return jnp.concatenate([total_a, total_b], axis=0).astype(BF16)

    return shards


def solution(mesh):
    return jax.shard_map(
        make_shards(mesh.shape["gy"]),
        mesh=mesh,
        in_specs=(P(("groups", "gy"), "gx"), P("gx", "gy"), P("gx", "gy"), P("gy", "gx")),
        out_specs=P(("groups", "gy"), "gx"),
        check_vma=False,
    )
```
